768 devices in a mesh: nodes: 96 (over x, z, core), cols: 8 (over y).
Axes of the slice: x: 4, y: 8, z: 12, core: 2. Of those that a mesh axis runs over, the one named last changes fastest.
Arguments:
- features: bfloat16 [98304, 1024], P('nodes'), may hold values from -6 to 6
- w_self: bfloat16 [1024, 1024], P(None, 'cols'), may hold values from -1 to 1
- w_neigh: bfloat16 [1024, 1024], P(None, 'cols'), may hold values from -1 to 1
- local_nbr: int32 [98304, 8], P('nodes'), may hold values from 0 to 1023
- hub_link: int32 [98304, 4], P('nodes'), may hold values from 0 to 767
- hub_used: int32 [98304, 4], P('nodes'), may hold values 0 or 1
- cotangent: bfloat16 [98304, 1024], P('nodes', 'cols'), may hold values from -0.046875 to 0.046875
Outputs:
- output: bfloat16 [98304, 1024], P('nodes', 'cols')
- grad_self: float32 [1024, 1024], P(None, 'cols')
- grad_neigh: float32 [1024, 1024], P(None, 'cols')
The draws below stay inside these ranges and needn't reach their ends.
All inputs are finite; a program needn't handle non-finite values. No bound on the sum of `hub_used` on one device may be relied on, other than what follows from the above.
Results may differ from the reference program's by a relative error of at most 0.007.
Values may be sent and summed in bfloat16 or wider, within the bound.
A program may use at most 32 MiB of HBM per device.

```python
import math
import jax
import jax.numpy as jnp
import numpy as np
from jax import lax

D = 1024
NODE_DEV = 1024
HUB_DEV = 8
FAN = 8
HFAN = 4
NODES = 98304
HUBS = 768


def column_scales(key):
    spread = jax.random.uniform(key, (D,), jnp.float32)
    place = jnp.arange(D, dtype=jnp.float32) / D
    return 10.0 ** (0.5 * place + 0.5 * spread - 0.75)


def scaled_weight(values, scales):
    return (values * scales[None, :] / math.sqrt(D)).astype(jnp.bfloat16)


def draw_features(key, part):
    key = jax.random.fold_in(key, 21)
    offset_key = jax.random.fold_in(key, 1)
    noise_key = jax.random.fold_in(key, 2)
    offset = jnp.clip(jax.random.normal(offset_key, (D,), jnp.float32), -2.5, 2.5)
    noise = jnp.clip(jax.random.normal(noise_key, (NODES, D), jnp.float32), -3.0, 3.0)
    return jnp.clip(offset[None, :] + noise, -6.0, 6.0).astype(jnp.bfloat16)


def draw_w_self(key, part):
    scales = column_scales(key)
    key = jax.random.fold_in(key, 11)
    values = jax.random.uniform(key, (D, D), jnp.float32, -1.7320508, 1.7320508)
    return scaled_weight(values, scales)


def draw_w_neigh(key, part):
    scales = column_scales(key)
    key = jax.random.fold_in(key, 12)
    values = jax.random.uniform(key, (D, D), jnp.float32, -1.7320508, 1.7320508)
    return scaled_weight(values, scales)


def plant(values, stream_key, least, largest):
    extent = values.shape
    spot = [jax.random.randint(jax.random.fold_in(stream_key, axis), (), 0, extent[axis]) for axis in range(len(extent))]
    values = values.at[tuple(spot)].set(least)
    longest = extent.index(max(extent))
    spot[longest] = (spot[longest] + 1) % extent[longest]
    return values.at[tuple(spot)].set(largest)


def levels(key, dims, shards, smallest, top_value):
    def one(dim, shards_of):
        heights = jax.random.uniform(jax.random.fold_in(jax.random.fold_in(key, 6), dim), (shards_of,), jnp.float32, smallest / len(shards), top_value / len(shards))
        return jnp.repeat(jnp.exp(heights), dims[dim] // shards_of).reshape((-1,) + (1,) * (len(dims) - dim - 1))

    gain = one(*shards[0])
    for cut in shards[1:]:
        gain = gain * one(*cut)
    return gain


def rank_bounds(amount, lean):
    loads = [(1 << 20) // math.isqrt(standing ** lean) + 1 for standing in range(1, amount + 1)]
    scale = 1 + sum(loads) // (1 << 30)
    return np.cumsum(np.array([max(1, weight // scale) for weight in loads]))


def ranked(key, extent, number_of, slope):
    table = rank_bounds(number_of, slope)
    ticket = jax.random.randint(jax.random.fold_in(key, 1), extent, 0, int(table[number_of - 1]))
    rank = jnp.searchsorted(jnp.asarray(table, jnp.int32), ticket, side="right")
    return jax.random.permutation(jax.random.fold_in(key, 2), number_of)[rank].astype(jnp.int32)


def scatter_about(key, dims, deviation, most, shards=(), kind=jnp.bfloat16):
    array = jax.random.normal(key, dims, jnp.float32) * deviation
    if len(shards) > 0:
        array = levels(key, dims, shards, -0.22, 0.18) * array
    return jnp.clip(array, min=-most, max=most).astype(kind)


def setup_inputs(seed: int = 0) -> dict:
    seeds = jax.random.split(jax.random.key(seed), 8)
    return {
        "features": draw_features(jax.random.fold_in(seeds[7], 71), 0),
        "w_self": draw_w_self(jax.random.fold_in(seeds[7], 71), 0),
        "w_neigh": draw_w_neigh(jax.random.fold_in(seeds[7], 71), 0),
        "local_nbr": plant(jax.random.randint(seeds[3], (NODES, FAN), 0, NODE_DEV), jax.random.fold_in(seeds[3], 1), 0, NODE_DEV - 1).astype(jnp.int32),
        "hub_link": plant(ranked(seeds[4], (NODES, HFAN), HUBS, 2), jax.random.fold_in(seeds[4], 3), 0, HUBS - 1).astype(jnp.int32),
        "hub_used": plant((jax.random.randint(seeds[5], (NODES, HFAN), 0, 2) < 1).astype(jnp.int32), jax.random.fold_in(seeds[5], 1), 0, 1),
        "cotangent": scatter_about(seeds[6], (NODES, D), (NODES ** -0.5), 0.046875, ((0, 96), (1, 8))),
    }


epsilon = 1e-05

def hub_nodes_of(hub_link):
    return hub_link // HUB_DEV * NODE_DEV + hub_link % HUB_DEV

def aggregate_rows(values, local_global, hub_node, used_mask, transpose):
    total = jnp.zeros(values.shape, jnp.float32)
    for k in range(FAN):
        if transpose:
            total = total.at[local_global[:, k]].add(values)
        else:
            total = total + values[local_global[:, k]]
    for k in range(HFAN):
        link_weight = used_mask[:, k][:, None]
        total = total + values[hub_node[:, k]] * link_weight
        total = total.at[hub_node[:, k]].add(values * link_weight)
    return total

def reference(features, w_self, w_neigh, local_nbr, hub_link, hub_used, cotangent):
    node_total = features.shape[0]
    row_ids = jnp.arange(node_total, dtype=jnp.int32)
    local_global = local_nbr + (row_ids // NODE_DEV * NODE_DEV)[:, None]
    hub_node = hub_nodes_of(hub_link)
    used_mask = hub_used.astype(jnp.float32)
    count_in = jnp.zeros((node_total,), jnp.float32)
    for k in range(HFAN):
        count_in = count_in.at[hub_node[:, k]].add(used_mask[:, k])
    degree = FAN + lax.optimization_barrier(jnp.sum(used_mask, axis=1)) + count_in
    proj_self = jnp.dot(features, w_self, preferred_element_type=jnp.float32)
    proj_neigh = jnp.dot(features, w_neigh, preferred_element_type=jnp.float32).astype(jnp.bfloat16)
    neigh_mean = aggregate_rows(proj_neigh.astype(jnp.float32), local_global, hub_node, used_mask, False) / degree[:, None]
    pre_act = proj_self + neigh_mean
    sig_gate = jax.nn.sigmoid(pre_act)
    activated = pre_act * sig_gate
    row_scale = jnp.sqrt(lax.optimization_barrier(jnp.mean(activated * activated, axis=1)) + epsilon)
    normed = activated / row_scale[:, None]
    output = normed.astype(jnp.bfloat16)
    cot_values = cotangent.astype(jnp.float32)
    inner_mean = lax.optimization_barrier(jnp.mean(cot_values * normed, axis=1))
    act_slope = sig_gate * (1.0 + pre_act * (1.0 - sig_gate))
    grad_pre = (cot_values - normed * inner_mean[:, None]) / row_scale[:, None] * act_slope
    grad_low = grad_pre.astype(jnp.bfloat16)
    scaled_grad = (grad_pre / degree[:, None]).astype(jnp.bfloat16)
    back_agg = aggregate_rows(scaled_grad.astype(jnp.float32), local_global, hub_node, used_mask, True).astype(jnp.bfloat16)
    grad_self = jnp.dot(features.T, grad_low, preferred_element_type=jnp.float32)
    grad_neigh = jnp.dot(features.T, back_agg, preferred_element_type=jnp.float32)
    return (output, grad_self, grad_neigh)
```

```python
import functools

import jax
import jax.numpy as jnp
from jax import lax
from jax.experimental import pallas as pl
from jax.experimental.pallas import tpu as pltpu
from jax.sharding import PartitionSpec as P

HUB_DEV = 8
FAN = 8
HFAN = 4
CORES = 2
GROUP_ROWS = 128
CHUNK = 256
EPSILON = 1e-05
X_CHIPS = 4

F32 = jnp.float32
BF16 = jnp.bfloat16
TALL = (((0,), (0,)), ((), ()))
WIDE = (((1,), (1,)), ((), ()))


def kernel(
    dims,
    feat,
    w_self,
    w_neigh,
    nbr,
    link,
    used,
    cot,
    out,
    grads,
    onehot,
    proj_self,
    proj_neigh,
    hub_rows,
    near,
    pre_act,
    push,
    push_in,
    zsend,
    zsend_in,
    own_p,

    own_sum,
    row_sums,
    low_grads,
    push2,
    push2_in,
    zsend2,
    zsend2_in,
    part,
    part_in,
    total,
    xsend,
    xsend_in,
    quarter,
    zq,
    zq_in,
    qfull,
    final,
    sems_z,
    sems_g,
    sems_y,
    sem_d,
    sems_x,
):
    xs, zs, ys = dims
    nodes, depth = feat.shape
    width = w_self.shape[1]
    hubs_z = zs * HUB_DEV
    groups = xs * CORES
    owners = 2 * zs // 3
    q_rows = depth // xs
    o_rows = q_rows // owners
    me = lax.axis_index("nodes")
    y = lax.axis_index("cols")
    c = lax.rem(me, CORES)
    z = lax.rem(me // CORES, zs)
    x = me // (CORES * zs)
    g = x * CORES + c

    def node(px, pz, pc):
        return (px * zs + pz) * CORES + pc

    def copy(src, dst, sems, row, slot, target):
        return pltpu.make_async_remote_copy(
            src_ref=src,
            dst_ref=dst,
            send_sem=sems.at[0, row, slot],
            recv_sem=sems.at[1, row, slot],
            device_id=target,
            device_id_type=pl.DeviceIdType.MESH,
        )

    def each(count, body):
        def step(k, carry):
            body(k)
            return carry

        lax.fori_loop(1, count, step, 0)

    def z_peer(k):
        pz = lax.rem(z + k, zs)
        return pz, (node(x, pz, c), y)

    def g_peer(k):
        px = lax.rem(x + k // CORES, xs)
        pc = lax.rem(c + lax.rem(k, CORES), CORES)
        return px * CORES + pc, (node(px, z, pc), y)

    def y_peer(k):
        return me, lax.rem(y + k, ys)

    def x_peer(k):
        px = lax.rem(x + k, xs)
        return px, (node(px, z, c), y)

    partner = (node(x, z, 1 - c), y)

    hub_rows[...] = jnp.zeros_like(hub_rows)
    barrier = pltpu.get_barrier_semaphore()

    def greet(target):
        pl.semaphore_signal(barrier, inc=1, device_id=target, device_id_type=pl.DeviceIdType.MESH)

    each(zs, lambda k: greet(z_peer(k)[1]))
    each(groups, lambda k: greet(g_peer(k)[1]))
    each(ys, lambda k: greet(y_peer(k)))

    own_p[z] = jnp.dot(feat[0:16, :], w_neigh[...], preferred_element_type=F32)[0:HUB_DEV]

    hub = link[...]
    place = hub % HUB_DEV
    device = hub // HUB_DEV
    core = device % CORES
    chip = device // CORES
    hub_x = jnp.zeros_like(chip)
    for i in range(1, xs):
        hub_x = hub_x + (chip >= i * zs).astype(jnp.int32)
    hub_z = chip - hub_x * zs
    column = (hub_x * CORES + core) * GROUP_ROWS + hub_z * HUB_DEV + place
    column = jnp.where(used[...] > 0, column, -1)
    link_base = nodes

    def build(first, count, picks, base):
        tile = 32

        def step(i, carry):
            row = i * tile
            ids = lax.broadcasted_iota(jnp.int32, (tile, nodes), 0) + row
            acc = jnp.zeros((tile, nodes), F32)
            for k in range(picks.shape[0]):
                acc = acc + jnp.where(ids == picks[k : k + 1, :], 1.0, 0.0)
            onehot[pl.ds(pl.multiple_of(base + row, tile), tile), :] = acc.astype(BF16)
            return carry

        lax.fori_loop(0, count // tile, step, 0)

    link_cols = groups * GROUP_ROWS
    build(0, link_cols, column, link_base)

    node_ones = jnp.ones((HUB_DEV, nodes), BF16)
    slice_cols = pl.ds(pl.multiple_of(y * width, 128), width)

    def push_step(i, carry):
        rows = onehot[pl.ds(pl.multiple_of(link_base + i * GROUP_ROWS, GROUP_ROWS), GROUP_ROWS), :]
        push[i] = jnp.dot(rows, feat[:, slice_cols], preferred_element_type=F32)
        push[i, hubs_z : hubs_z + HUB_DEV, 0:GROUP_ROWS] = lax.dot_general(
            node_ones, rows, WIDE, preferred_element_type=F32
        )
        return carry

    lax.fori_loop(0, groups, push_step, 0)

    pl.semaphore_wait(barrier, zs + groups + ys - 3)

    ap_z = lambda k: copy(own_p.at[z], own_p.at[z], sems_z, 0, k - 1, z_peer(k)[1])

    def pushx(k):
        pg, target = g_peer(k)
        return copy(
            push.at[pg, pl.ds(0, hubs_z + HUB_DEV)], push_in.at[k - 1], sems_g, 0, k - 1, target
        )

    each(zs, lambda k: ap_z(k).start())
    each(groups, lambda k: pushx(k).start())

    def proj_step(i, carry):
        rows = pl.ds(pl.multiple_of(i * CHUNK, CHUNK), CHUNK)
        both = jnp.dot(
            feat[rows, :],
            jnp.concatenate([w_self[...], w_neigh[...]], axis=1),
            preferred_element_type=F32,
        )
        proj_self[rows, :] = both[:, :width]
        proj_neigh[rows, :] = both[:, width:].astype(BF16)
        return carry

    lax.fori_loop(0, nodes // CHUNK, proj_step, 0)

    each(zs, lambda k: ap_z(k).wait())
    plane_rows = own_p[...].reshape(hubs_z, width).astype(BF16)
    hub_rows[g, 0:hubs_z] = plane_rows

    def ap_x(k):
        pg, target = g_peer(k)
        mine = hub_rows.at[g, pl.ds(0, hubs_z)]
        return copy(mine, mine, sems_g, 1, k - 1, target)

    each(groups, lambda k: ap_x(k).start())

    each(groups, lambda k: pushx(k).wait())
    summed = push[g, 0 : hubs_z + HUB_DEV]
    for k in range(groups - 1):
        summed = summed + push_in[k]
    for i in range(zs):
        zsend[i, 0:HUB_DEV] = summed[i * HUB_DEV : (i + 1) * HUB_DEV]
        zsend[i, HUB_DEV : 2 * HUB_DEV] = summed[hubs_z : hubs_z + HUB_DEV]

    def pushz(k):
        pz, target = z_peer(k)
        return copy(zsend.at[pz], zsend_in.at[k - 1], sems_z, 1, k - 1, target)

    each(zs, lambda k: pushz(k).start())

    build(0, nodes, nbr[...], 0)

    def near_step(i, carry):
        cols = pl.ds(pl.multiple_of(i * CHUNK, CHUNK), CHUNK)
        near[cols, :] = lax.dot_general(
            onehot[0:nodes, cols], proj_neigh[...], TALL, preferred_element_type=F32
        )
        return carry

    lax.fori_loop(0, nodes // CHUNK, near_step, 0)

    each(zs, lambda k: pushz(k).wait())
    hub_sum = zsend[z]
    for k in range(zs - 1):
        hub_sum = hub_sum + zsend_in[k]
    own_sum[y] = hub_sum[0:HUB_DEV]
    count_block = hub_sum[HUB_DEV : 2 * HUB_DEV]
    lane = lax.broadcasted_iota(jnp.int32, count_block.shape, 1)
    sub = lax.broadcasted_iota(jnp.int32, count_block.shape, 0)
    count_in = jnp.sum(
        jnp.where(lane == sub + z * HUB_DEV, count_block, 0.0), axis=1, keepdims=True
    )
    sum_y = lambda k: copy(own_sum.at[y], own_sum.at[y], sems_y, 0, k - 1, y_peer(k))
    each(ys, lambda k: sum_y(k).start())

    each(groups, lambda k: ap_x(k).wait())
    pulled_rhs = jnp.concatenate(
        [hub_rows[...].reshape(link_cols, width), jnp.ones((link_cols, width), BF16)], axis=1
    )

    def pull_step(i, carry):
        cols = pl.ds(pl.multiple_of(i * CHUNK, CHUNK), CHUNK)
        both = lax.dot_general(
            onehot[pl.ds(link_base, link_cols), cols],
            pulled_rhs,
            TALL,
            preferred_element_type=F32,
        )
        near[cols, :] = near[cols, :] + both[:, :width]
        pre_act[cols, :] = FAN + both[:, width:]
        return carry

    lax.fori_loop(0, nodes // CHUNK, pull_step, 0)

    each(ys, lambda k: sum_y(k).wait())
    linked = jnp.concatenate([own_sum[i] for i in range(ys)], axis=1)
    linked_high = linked.astype(BF16).astype(F32)
    linked_low = linked - linked_high
    inflow = jnp.dot(
        jnp.concatenate([linked_high, linked_low], axis=0).astype(BF16),
        w_neigh[...],
        preferred_element_type=F32,
    )
    near[0:HUB_DEV, :] = near[0:HUB_DEV, :] + (inflow[0:HUB_DEV] + inflow[HUB_DEV:])
    pre_act[0:HUB_DEV, :] = pre_act[0:HUB_DEV, :] + count_in

    chunks = nodes // CHUNK
    lanes = lax.broadcasted_iota(jnp.int32, (2 * chunks, width), 0)
    sums = jnp.zeros((2 * chunks, CHUNK), F32)
    for i in range(chunks):
        rows = slice(i * CHUNK, (i + 1) * CHUNK)
        degree = pre_act[rows, :]
        pre = proj_self[rows, :] + near[rows, :] / degree
        act = pre * jax.nn.sigmoid(pre)
        near[rows, :] = degree
        pre_act[rows, :] = pre
        for at, value in ((i, act * act), (chunks + i, act * cot[rows, :].astype(F32))):
            sums = sums + lax.dot_general(
                jnp.where(lanes == at, 1.0, 0.0),
                value,
                WIDE,
                preferred_element_type=F32,
                precision=lax.Precision.HIGHEST,
            )
    row_sums[y] = sums
    sum_c = lambda k: copy(row_sums.at[y], row_sums.at[y], sems_y, 1, k - 1, y_peer(k))
    each(ys, lambda k: sum_c(k).start())
    each(ys, lambda k: sum_c(k).wait())
    sums = row_sums[0]
    for i in range(1, ys):
        sums = sums + row_sums[i]
    inv_scale = 1.0 / jnp.sqrt(sums[0:chunks] / depth + EPSILON)
    inner = sums[chunks:] * inv_scale / depth
    by_row = jnp.transpose(jnp.concatenate([inv_scale, inner], axis=0))

    for i in range(chunks):
        rows = slice(i * CHUNK, (i + 1) * CHUNK)
        pre = pre_act[rows, :]
        sig = jax.nn.sigmoid(pre)
        inv = by_row[:, i : i + 1]
        normed = pre * sig * inv
        out[rows, :] = normed.astype(BF16)
        slope = sig * (1.0 + pre * (1.0 - sig))
        grad = (cot[rows, :].astype(F32) - normed * by_row[:, chunks + i : chunks + i + 1]) * inv * slope
        low_grads[rows, 0:width] = grad.astype(BF16)
        low_grads[rows, width:] = (grad / near[rows, :]).astype(BF16)

    def push2_step(i, carry):
        push2[i] = jnp.dot(
            onehot[pl.ds(pl.multiple_of(link_base + i * GROUP_ROWS, GROUP_ROWS), GROUP_ROWS), :],
            low_grads[:, width:],
            preferred_element_type=F32,
        )
        return carry

    lax.fori_loop(0, groups, push2_step, 0)

    def push2x(k):
        pg, target = g_peer(k)
        return copy(push2.at[pg, pl.ds(0, hubs_z)], push2_in.at[k - 1], sems_g, 2, k - 1, target)

    each(groups, lambda k: push2x(k).start())
    own_scaled = low_grads[0:16, width:].astype(F32)[0:HUB_DEV]

    def part_step(which):
        def step(i, carry):
            cols = pl.ds(pl.multiple_of(i * CHUNK, CHUNK), CHUNK)
            part[which, cols, :] = lax.dot_general(
                feat[:, cols],
                low_grads[:, which * width : (which + 1) * width],
                TALL,
                preferred_element_type=F32,
            )
            return carry

        lax.fori_loop(0, depth // CHUNK, step, 0)

    part_step(0)
    swap = pltpu.make_async_remote_copy(
        src_ref=part.at[1 - c],
        dst_ref=part_in,
        send_sem=sem_d.at[0],
        recv_sem=sem_d.at[1],
        device_id=partner,
        device_id_type=pl.DeviceIdType.MESH,
    )

    @pl.when(c == 1)
    def _():
        swap.start()

    def back_step(i, carry):
        rows = pl.ds(pl.multiple_of(i * CHUNK, CHUNK), CHUNK)
        near[rows, :] = jnp.dot(onehot[rows, :], low_grads[:, width:], preferred_element_type=F32)
        return carry

    lax.fori_loop(0, nodes // CHUNK, back_step, 0)

    each(groups, lambda k: push2x(k).wait())
    summed = push2[g, 0:hubs_z]
    for k in range(groups - 1):
        summed = summed + push2_in[k]
    zsend2[...] = summed.reshape(zs, HUB_DEV, width)

    def push2z(k):
        pz, target = z_peer(k)
        return copy(zsend2.at[pz], zsend2_in.at[k - 1], sems_z, 2, k - 1, target)

    each(zs, lambda k: push2z(k).start())

    low_grads[:, width:] = near[...].astype(BF16)
    part_step(1)

    def sendx(k):
        px, target = x_peer(k)
        return copy(xsend.at[px], xsend_in.at[k - 1], sems_x, 0, k - 1, target)

    def open_x():
        swap.wait_recv()
        for i in range(xs):
            rows = slice(i * q_rows, (i + 1) * q_rows)
            both = part[c, rows, :] + part_in[rows, :]
            total[i] = both
            xsend[i] = both.astype(BF16)
        each(xs, lambda k: sendx(k).start())

    @pl.when(c == 0)
    def _():
        open_x()

    each(zs, lambda k: push2z(k).wait())
    back = zsend2[z]
    for k in range(zs - 1):
        back = back + zsend2_in[k]
    back_high = back.astype(BF16).astype(F32)
    own_feat = feat[0:16, :].astype(F32)[0:HUB_DEV]
    tall = jnp.concatenate([own_feat, own_feat, linked_high, linked_low], axis=0).astype(BF16)
    flat = jnp.concatenate([back_high, back - back_high, own_scaled, own_scaled], axis=0).astype(BF16)
    part[1] = part[1] + lax.dot_general(tall, flat, TALL, preferred_element_type=F32)

    @pl.when(c == 0)
    def _():
        swap.start()

    @pl.when(c == 1)
    def _():
        open_x()

    each(xs, lambda k: sendx(k).wait())
    reduced = total[x]
    for k in range(xs - 1):
        reduced = reduced + xsend_in[k].astype(F32)
    quarter[...] = reduced.reshape(owners, o_rows, width)
    zq[...] = reduced.astype(BF16).reshape(owners, o_rows, width)

    def owns(pz):
        return lax.rem(pz, 3) != 2

    def rank(pz):
        return (pz // 3) * 2 + lax.rem(pz, 3)

    def sendq(k):
        pz, target = z_peer(k)
        return copy(zq.at[rank(pz)], zq_in.at[k - 1], sems_z, 3, k - 1, target)

    def start_q(k):
        @pl.when(owns(z_peer(k)[0]))
        def _():
            sendq(k).start()

    each(zs, start_q)

    def sendf(k):
        _, target = z_peer(k)
        mine = qfull.at[rank(z)]
        return copy(mine, mine, sems_z, 4, k - 1, target)

    waitq = lambda k: copy(zq.at[0], zq_in.at[k - 1], sems_z, 3, k - 1, z_peer(k)[1])
    waitf = lambda k: copy(qfull.at[0], qfull.at[0], sems_z, 4, k - 1, z_peer(k)[1])

    @pl.when(owns(z))
    def _():
        each(zs, lambda k: waitq(k).wait_recv())
        mine = quarter[rank(z)]
        for k in range(zs - 1):
            mine = mine + zq_in[k].astype(F32)
        qfull[rank(z)] = mine.astype(BF16)
        each(zs, lambda k: sendf(k).start())

    def finish_q(k):
        @pl.when(owns(z_peer(k)[0]))
        def _():
            waitq(k).wait_send()

        @pl.when(owns(lax.rem(z + zs - k, zs)))
        def _():
            waitf(k).wait_recv()

    each(zs, finish_q)
    final[c, x] = qfull[...].reshape(q_rows, width)

    def sendq_x(k):
        _, target = x_peer(k)
        mine = final.at[c, x]
        return copy(mine, mine, sems_x, 1, k - 1, target)

    def forward(k):
        px = lax.rem(x + xs - k, xs)
        piece = final.at[c, px]
        return copy(piece, piece, sems_x, 2, k, partner)

    each(xs, lambda k: sendq_x(k).start())
    forward(0).start()

    def pass_on(k):
        sendq_x(k).wait_recv()
        forward(k).start()

    each(xs, pass_on)
    forward(0).wait()
    each(xs, lambda k: forward(k).wait())
    each(xs, lambda k: sendq_x(k).wait_send())
    swap.wait_send()

    @pl.when(owns(z))
    def _():
        each(zs, lambda k: waitf(k).wait_send())

    grads[...] = final[...].reshape(CORES, depth, width)


def local(dims, features, w_self, w_neigh, local_nbr, hub_link, hub_used, cotangent):
    xs, zs, ys = dims
    nodes, depth = features.shape
    width = w_self.shape[1]
    groups = xs * CORES
    hubs_z = zs * HUB_DEV
    owners = 2 * zs // 3
    q_rows = depth // xs
    o_rows = q_rows // owners
    link_cols = groups * GROUP_ROWS
    vmem = pltpu.VMEM
    scratch = [
        vmem((nodes + link_cols, nodes), BF16),
        vmem((nodes, width), F32),
        vmem((nodes, width), BF16),
        vmem((groups, GROUP_ROWS, width), BF16),
        vmem((nodes, width), F32),
        vmem((nodes, width), F32),
        vmem((groups, GROUP_ROWS, width), F32),
        vmem((groups - 1, hubs_z + HUB_DEV, width), F32),
        vmem((zs, 2 * HUB_DEV, width), F32),
        vmem((zs - 1, 2 * HUB_DEV, width), F32),
        vmem((zs, HUB_DEV, width), F32),

        vmem((ys, HUB_DEV, width), F32),
        vmem((ys, 2 * (nodes // CHUNK), CHUNK), F32),
        vmem((nodes, 2 * width), BF16),
        vmem((groups, GROUP_ROWS, width), F32),
        vmem((groups - 1, hubs_z, width), F32),
        vmem((zs, HUB_DEV, width), F32),
        vmem((zs - 1, HUB_DEV, width), F32),
        vmem((CORES, depth, width), F32),
        vmem((depth, width), F32),
        vmem((xs, q_rows, width), F32),
        vmem((xs, q_rows, width), BF16),
        vmem((xs - 1, q_rows, width), BF16),
        vmem((owners, o_rows, width), F32),
        vmem((owners, o_rows, width), BF16),
        vmem((zs - 1, o_rows, width), BF16),
        vmem((owners, o_rows, width), BF16),
        vmem((CORES, xs, q_rows, width), BF16),
        pltpu.SemaphoreType.DMA((2, 5, zs - 1)),
        pltpu.SemaphoreType.DMA((2, 3, groups - 1)),
        pltpu.SemaphoreType.DMA((2, 2, ys - 1)),
        pltpu.SemaphoreType.DMA((2,)),
        pltpu.SemaphoreType.DMA((2, 3, xs)),
    ]
    whole = pl.BlockSpec(memory_space=pltpu.VMEM)
    output, grads = pl.pallas_call(
        functools.partial(kernel, dims),
        out_shape=(
            jax.ShapeDtypeStruct((nodes, width), BF16),
            jax.ShapeDtypeStruct((CORES, depth, width), BF16),
        ),
        in_specs=[whole] * 7,
        out_specs=(whole, whole),
        scratch_shapes=scratch,
        compiler_params=pltpu.CompilerParams(
            collective_id=0, has_side_effects=True, vmem_limit_bytes=56 * 1024 * 1024
        ),
    )(features, w_self, w_neigh, local_nbr.T, hub_link.T, hub_used.T, cotangent)
    return output, grads[0].astype(F32), grads[1].astype(F32)


def solution(mesh):
    ys = mesh.shape["cols"]
    xs = X_CHIPS
    zs = mesh.shape["nodes"] // (xs * CORES)
    placed = (
        P("nodes", None),
        P(None, "cols"),
        P(None, "cols"),
        P("nodes", None),
        P("nodes", None),
        P("nodes", None),
        P("nodes", "cols"),
    )
    return jax.shard_map(
        functools.partial(local, (xs, zs, ys)),
        mesh=mesh,
        in_specs=placed,
        out_specs=(P("nodes", "cols"), P(None, "cols"), P(None, "cols")),
        check_vma=False,
    )
```

```python
import functools
import types

import jax
import jax.numpy as jnp
from jax import lax
from jax.experimental import pallas as pl
from jax.experimental.pallas import tpu as pltpu
from jax.sharding import PartitionSpec as P

HUB_DEV = 8
FAN = 8
CORES = 2
GROUP_ROWS = 128
CHUNK = 256
TILE = 32
EPSILON = 1e-05
X_CHIPS = 4

F32 = jnp.float32
BF16 = jnp.bfloat16
TALL = (((0,), (0,)), ((), ()))
WIDE = (((1,), (1,)), ((), ()))


def sizes(dims, nodes, depth, width):
    xs, zs, ys = dims
    s = types.SimpleNamespace(xs=xs, zs=zs, ys=ys, nodes=nodes, depth=depth, width=width)
    s.groups = xs * CORES
    s.hubs_z = zs * HUB_DEV
    s.owners = 2 * zs // 3
    s.q_rows = depth // xs
    s.o_rows = s.q_rows // s.owners
    s.link_cols = s.groups * GROUP_ROWS
    s.chunks = nodes // CHUNK
    return s


def scratch_of(s):
    vmem = pltpu.VMEM
    dma = pltpu.SemaphoreType.DMA
    w = s.width
    sum_rows = 2 * s.chunks
    hub_k = 2 * s.hubs_z + 2 * HUB_DEV
    return {
        "feat": vmem((s.nodes, s.depth), BF16),
        "w_self": vmem((s.depth, w), BF16),
        "w_neigh": vmem((s.depth, w), BF16),
        "nbr": vmem((FAN, s.nodes), jnp.int32),
        "link": vmem((4, s.nodes), jnp.int32),
        "used": vmem((4, s.nodes), jnp.int32),
        "cot": vmem((s.nodes, w), BF16),
        "links": vmem((s.link_cols, s.nodes), BF16),
        "locals_": vmem((s.nodes, s.nodes), BF16),
        "proj_self": vmem((s.nodes, w), F32),
        "pushable": vmem((s.nodes, 2 * w), BF16),
        "hub_rows": vmem((s.groups, GROUP_ROWS, w), BF16),
        "near": vmem((s.nodes, w), F32),
        "degree": vmem((s.nodes, w), F32),
        "pre_act": vmem((s.nodes, w), F32),
        "push": vmem((s.groups, s.hubs_z, 2 * w), F32),
        "push_p": vmem((s.groups, s.hubs_z + 16, w), BF16),
        "push_p_in": vmem((s.groups - 1, s.hubs_z + 16, w), BF16),
        "push_g": vmem((s.groups, s.hubs_z, w), BF16),
        "push_g_in": vmem((s.groups - 1, s.hubs_z, w), BF16),
        "zsend_p": vmem((s.zs, 2 * HUB_DEV, w), F32),
        "zsend_p_in": vmem((s.zs - 1, 2 * HUB_DEV, w), F32),
        "zsend_g": vmem((s.zs, HUB_DEV, w), F32),
        "zsend_g_in": vmem((s.zs - 1, HUB_DEV, w), F32),
        "own_p": vmem((s.zs, HUB_DEV, w), F32),
        "own_sum": vmem((s.ys, HUB_DEV, w), F32),
        "hub_feat": vmem((s.zs, 2 * HUB_DEV, s.depth // 2), BF16),
        "sums_a": vmem((s.ys, sum_rows, CHUNK), F32),
        "sums_b": vmem((s.ys, sum_rows, CHUNK), F32),
        "low": vmem((s.nodes, w), BF16),
        "scaled": vmem((s.nodes, w), BF16),
        "back": vmem((s.nodes, w), F32),
        "back_low": vmem((s.nodes, w), BF16),
        "push2": vmem((s.groups, GROUP_ROWS, w), F32),
        "push2_low": vmem((s.groups, s.hubs_z, w), BF16),
        "push2_in": vmem((s.groups - 1, s.hubs_z, w), BF16),
        "tall": vmem((hub_k, s.depth), BF16),
        "part": vmem((CORES, s.xs, s.q_rows, w), F32),
        "part_in": vmem((s.xs, s.q_rows, w), F32),
        "total": vmem((s.q_rows, w), F32),
        "xsend": vmem((s.xs, s.q_rows, w), BF16),
        "xsend_in": vmem((s.xs - 1, s.q_rows, w), BF16),
        "quarter": vmem((s.owners, s.o_rows, w), F32),
        "zq": vmem((s.owners, s.o_rows, w), BF16),
        "zq_in": vmem((s.zs - 1, s.o_rows, w), BF16),
        "final": vmem((CORES, s.xs, s.owners, s.o_rows, w), BF16),
        "sems_z": dma((2, 6, s.zs - 1)),
        "sems_g": dma((2, 4, s.groups - 1)),
        "sems_y": dma((2, 3, s.ys - 1)),
        "sems_x": dma((2, 3, s.xs)),
        "sems_f": dma((2, s.xs - 1, s.owners)),
        "sems_l": dma((7,)),
    }


def kernel(s, names, feat_in, w_self_in, w_neigh_in, nbr_in, link_in, used_in, cot_in, out, grads, *refs):
    r = types.SimpleNamespace(**dict(zip(names, refs)))
    xs, zs, ys, width, nodes = s.xs, s.zs, s.ys, s.width, s.nodes
    groups, hubs_z, owners, q_rows = s.groups, s.hubs_z, s.owners, s.q_rows
    chunks = s.chunks
    me = lax.axis_index("nodes")
    y = lax.axis_index("cols")
    c = lax.rem(me, CORES)
    z = lax.rem(me // CORES, zs)
    x = me // (CORES * zs)
    g = x * CORES + c

    def node(px, pz, pc):
        return (px * zs + pz) * CORES + pc

    def copy(src, dst, sems, row, slot, target):
        return pltpu.make_async_remote_copy(
            src_ref=src,
            dst_ref=dst,
            send_sem=sems.at[0, row, slot],
            recv_sem=sems.at[1, row, slot],
            device_id=target,
            device_id_type=pl.DeviceIdType.MESH,
        )

    def loop(count, body):
        def step(i, carry):
            body(i)
            return carry

        lax.fori_loop(0, count, step, 0)

    def ranked(count, i):
        return count // 2 + (i // 2) * (1 - 2 * lax.rem(i, 2))

    def each(count, body):
        loop(count - 1, lambda i: body(ranked(count, i + 1)))

    def each_near(count, body):
        loop(count - 1, lambda i: body(ranked(count, count - 1 - i)))

    def z_peer(k):
        pz = lax.rem(z + k, zs)
        return pz, (node(x, pz, c), y)

    def g_peer(k):
        px = lax.rem(x + k // CORES, xs)
        pc = lax.rem(c + lax.rem(k, CORES), CORES)
        return px * CORES + pc, (node(px, z, pc), y)

    def y_peer(k):
        return me, lax.rem(y + k, ys)

    def x_peer(k):
        px = lax.rem(x + k, xs)
        return px, (node(px, z, c), y)

    partner = (node(x, z, 1 - c), y)

    barrier = pltpu.get_barrier_semaphore()

    def greet(target):
        pl.semaphore_signal(barrier, inc=1, device_id=target, device_id_type=pl.DeviceIdType.MESH)

    each(zs, lambda k: greet(z_peer(k)[1]))
    each(ys, lambda k: greet(y_peer(k)))
    each(groups, lambda k: greet(g_peer(k)[1]))
    inputs = [
        pltpu.make_async_copy(src, dst, r.sems_l.at[i])
        for i, (src, dst) in enumerate(
            (
                (link_in, r.link),
                (used_in, r.used),
                (w_neigh_in, r.w_neigh),
                (feat_in, r.feat),
                (w_self_in, r.w_self),
                (nbr_in, r.nbr),
                (cot_in, r.cot),
            )
        )
    ]
    for item in inputs:
        item.start()
    r.hub_rows[:, hubs_z:] = jnp.zeros((groups, GROUP_ROWS - hubs_z, width), BF16)

    def build(dest, base, count, picks):
        for first in range(0, count, TILE):
            ids = lax.broadcasted_iota(jnp.int32, (TILE, nodes), 0) + (base + first)
            acc = jnp.zeros((TILE, nodes), F32)
            for k in range(picks.shape[0]):
                acc = acc + jnp.where(ids == picks[k : k + 1, :], 1.0, 0.0)
            dest[pl.ds(pl.multiple_of(base + first, TILE), TILE), :] = acc.astype(BF16)

    inputs[0].wait()
    inputs[1].wait()
    hub = r.link[...]
    place = lax.rem(hub, HUB_DEV)
    device = lax.div(hub, HUB_DEV)
    core = lax.rem(device, CORES)
    chip = lax.div(device, CORES)
    hub_x = jnp.zeros_like(chip)
    for i in range(1, xs):
        hub_x = hub_x + (chip >= i * zs).astype(jnp.int32)
    hub_z = chip - hub_x * zs
    column = (hub_x * CORES + core) * GROUP_ROWS + hub_z * HUB_DEV + place
    r.link[...] = jnp.where(r.used[...] > 0, column, -1)
    tiles = -(-hubs_z // TILE) * TILE

    def build_links(i):
        base = i * GROUP_ROWS
        build(r.links, base, tiles, r.link[...])
        if tiles < GROUP_ROWS:
            rest = GROUP_ROWS - tiles
            r.links[pl.ds(pl.multiple_of(base + tiles, TILE), rest), :] = jnp.zeros((rest, nodes), BF16)

    loop(groups, build_links)

    inputs[2].wait()
    inputs[3].wait()
    own_rows = r.feat[0:16, :]
    r.own_p[z] = jnp.dot(own_rows, r.w_neigh[...], preferred_element_type=F32)[0:HUB_DEV]
    pl.semaphore_wait(barrier, zs + groups + ys - 3)

    def gather_z(k):
        mine = r.own_p.at[z]
        return copy(mine, mine, r.sems_z, 0, k - 1, z_peer(k)[1])

    each(zs, lambda k: gather_z(k).start())

    def proj_step(i):
        rows = pl.ds(pl.multiple_of(i * CHUNK, CHUNK), CHUNK)
        r.pushable[rows, 0:width] = jnp.dot(
            r.feat[rows, :], r.w_neigh[...], preferred_element_type=F32
        ).astype(BF16)
        r.pushable[rows, width:] = r.feat[rows, pl.ds(pl.multiple_of(y * width, 128), width)]

    loop(chunks, proj_step)
    node_ones = jnp.ones((HUB_DEV, nodes), BF16)

    def push_p(pg, k):
        target = g_peer(k)[1]
        return copy(r.push_p.at[pg], r.push_p_in.at[k - 1], r.sems_g, 0, k - 1, target)

    def push_g(pg, k):
        target = g_peer(k)[1]
        return copy(r.push_g.at[pg], r.push_g_in.at[k - 1], r.sems_g, 1, k - 1, target)

    def push_rows(pg):
        rows = r.links[pl.ds(pl.multiple_of(pg * GROUP_ROWS, GROUP_ROWS), GROUP_ROWS), :]
        both = jnp.dot(rows, r.pushable[...], preferred_element_type=F32)[0:hubs_z]
        count = lax.dot_general(node_ones, rows, WIDE, preferred_element_type=F32)
        count_high = count.astype(BF16).astype(F32)
        counts = jnp.concatenate([count_high, count - count_high], axis=0)
        r.push[pg] = both
        r.push_p[pg, 0:hubs_z] = both[:, :width].astype(BF16)
        r.push_p[pg, hubs_z:] = counts.astype(BF16)
        r.push_g[pg] = both[:, width:].astype(BF16)

    def push_to(k):
        pg = g_peer(k)[0]
        push_rows(pg)
        push_p(pg, k).start()

    each(groups, push_to)
    push_rows(g)
    each(groups, lambda k: push_g(g_peer(k)[0], k).start())

    each(zs, lambda k: gather_z(k).wait())
    r.hub_rows[g, 0:hubs_z] = r.own_p[...].reshape(hubs_z, width).astype(BF16)

    def gather_g(k):
        mine = r.hub_rows.at[g, pl.ds(0, hubs_z)]
        return copy(mine, mine, r.sems_g, 2, k - 1, g_peer(k)[1])

    each(groups, lambda k: gather_g(k).start())

    inputs[5].wait()
    loop(nodes // 128, lambda i: build(r.locals_, i * 128, 128, r.nbr[...]))

    each(groups, lambda k: push_p(g_peer(k)[0], k).wait())
    summed = r.push[g, :, 0:width]
    counts = r.push_p[g, hubs_z:].astype(F32)
    for k in range(groups - 1):
        summed = summed + r.push_p_in[k, 0:hubs_z].astype(F32)
        counts = counts + r.push_p_in[k, hubs_z:].astype(F32)
    counts = counts[0:HUB_DEV] + counts[HUB_DEV:]
    for i in range(zs):
        r.zsend_p[i, 0:HUB_DEV] = summed[i * HUB_DEV : (i + 1) * HUB_DEV]
        r.zsend_p[i, HUB_DEV:] = counts

    def push_pz(k):
        pz, target = z_peer(k)
        return copy(r.zsend_p.at[pz], r.zsend_p_in.at[k - 1], r.sems_z, 1, k - 1, target)

    each(zs, lambda k: push_pz(k).start())

    inputs[4].wait()

    def near_step(i):
        rows = pl.ds(pl.multiple_of(i * CHUNK, CHUNK), CHUNK)
        r.proj_self[rows, :] = jnp.dot(r.feat[rows, :], r.w_self[...], preferred_element_type=F32)
        r.near[rows, :] = lax.dot_general(
            r.locals_[:, rows], r.pushable[:, 0:width], TALL, preferred_element_type=F32
        )

    loop(chunks, near_step)

    each(groups, lambda k: gather_g(k).wait())

    def pull_step(i):
        cols = pl.ds(pl.multiple_of(i * CHUNK, CHUNK), CHUNK)
        pulled_rhs = jnp.concatenate(
            [r.hub_rows[...].reshape(s.link_cols, width), jnp.ones((s.link_cols, width), BF16)],
            axis=1,
        )
        both = lax.dot_general(r.links[:, cols], pulled_rhs, TALL, preferred_element_type=F32)
        r.near[cols, :] = r.near[cols, :] + both[:, :width]
        r.degree[cols, :] = FAN + both[:, width:]

    loop(chunks, pull_step)

    inputs[6].wait()
    picks = lax.broadcasted_iota(jnp.int32, (2 * chunks, width), 0)

    def forward(i):
        rows = slice(i * CHUNK, (i + 1) * CHUNK)
        pre = r.proj_self[rows, :] + r.near[rows, :] / r.degree[rows, :]
        act = pre * jax.nn.sigmoid(pre)
        r.pre_act[rows, :] = pre
        sums = jnp.zeros((2 * chunks, CHUNK), F32)
        for at, value in ((i, act * act), (chunks + i, act * r.cot[rows, :].astype(F32))):
            sums = sums + lax.dot_general(
                jnp.where(picks == at, 1.0, 0.0),
                value,
                WIDE,
                preferred_element_type=F32,
                precision=lax.Precision.HIGHEST,
            )
        return sums

    def col_sum(buf, row):
        return lambda k: copy(buf.at[y], buf.at[y], r.sems_y, row, k - 1, y_peer(k))

    def by_row(buf):
        sums = buf[0]
        for i in range(1, ys):
            sums = sums + buf[i]
        inv_scale = 1.0 / jnp.sqrt(sums[0:chunks] / s.depth + EPSILON)
        inner = sums[chunks:] * inv_scale / s.depth
        return jnp.transpose(jnp.concatenate([inv_scale, inner], axis=0))

    def backward(i, scales):
        rows = slice(i * CHUNK, (i + 1) * CHUNK)
        pre = r.pre_act[rows, :]
        sig = jax.nn.sigmoid(pre)
        inv = scales[:, i : i + 1]
        inner = scales[:, chunks + i : chunks + i + 1]
        normed = pre * sig * inv
        out[rows, :] = normed.astype(BF16)
        slope = sig * (1.0 + pre * (1.0 - sig))
        grad = (r.cot[rows, :].astype(F32) - normed * inner) * inv * slope
        r.low[rows, :] = grad.astype(BF16)
        r.scaled[rows, :] = (grad / r.degree[rows, :]).astype(BF16)

    sums = forward(1)
    for i in range(2, chunks):
        sums = sums + forward(i)
    r.sums_a[y] = sums
    sum_a = col_sum(r.sums_a, 0)
    each(ys, lambda k: sum_a(k).start())

    each(groups, lambda k: push_g(g_peer(k)[0], k).wait())
    summed = r.push[g, :, width:]
    for k in range(groups - 1):
        summed = summed + r.push_g_in[k].astype(F32)
    r.zsend_g[...] = summed.reshape(zs, HUB_DEV, width)

    def push_gz(k):
        pz, target = z_peer(k)
        return copy(r.zsend_g.at[pz], r.zsend_g_in.at[k - 1], r.sems_z, 2, k - 1, target)

    each(zs, lambda k: push_gz(k).start())

    each(zs, lambda k: push_pz(k).wait())
    hub_sum = r.zsend_p[z]
    for k in range(zs - 1):
        hub_sum = hub_sum + r.zsend_p_in[k]
    count_block = hub_sum[HUB_DEV:]
    lane = lax.broadcasted_iota(jnp.int32, count_block.shape, 1)
    sub = lax.broadcasted_iota(jnp.int32, count_block.shape, 0)
    count_in = jnp.sum(
        jnp.where(lane == sub + z * HUB_DEV, count_block, 0.0), axis=1, keepdims=True
    )
    r.near[0:HUB_DEV, :] = r.near[0:HUB_DEV, :] + hub_sum[0:HUB_DEV]
    r.degree[0:HUB_DEV, :] = r.degree[0:HUB_DEV, :] + count_in
    r.sums_b[y] = forward(0)
    sum_b = col_sum(r.sums_b, 1)
    each(ys, lambda k: sum_b(k).start())

    own_f32 = r.feat[0:16, :].astype(F32)[0:HUB_DEV]
    half = s.depth // 2
    r.hub_feat[z] = jnp.concatenate([own_f32[:, :half], own_f32[:, half:]], axis=0).astype(BF16)

    def gather_f(k):
        mine = r.hub_feat.at[z]
        return copy(mine, mine, r.sems_z, 3, k - 1, z_peer(k)[1])

    each(zs, lambda k: gather_f(k).start())

    def products(lo, hi, first):
        span = slice(lo, hi)

        def add(ref, index, value):
            ref[index] = value if first else ref[index] + value

        def push_step(i):
            rows = pl.ds(pl.multiple_of(i * GROUP_ROWS, GROUP_ROWS), GROUP_ROWS)
            value = jnp.dot(r.links[rows, span], r.scaled[span, :], preferred_element_type=F32)
            add(r.push2, i, value)

        def back_step(i):
            rows = pl.ds(pl.multiple_of(i * CHUNK, CHUNK), CHUNK)
            value = jnp.dot(r.locals_[rows, span], r.scaled[span, :], preferred_element_type=F32)
            add(r.back, (rows, slice(None)), value)

        def self_step(q):
            cols = pl.ds(pl.multiple_of(q * q_rows, q_rows), q_rows)
            value = lax.dot_general(
                r.feat[span, cols], r.low[span, :], TALL, preferred_element_type=F32
            )
            add(r.part, (0, q), value)

        return push_step, back_step, self_step

    each(ys, lambda k: sum_a(k).wait())
    scales = by_row(r.sums_a)
    for i in range(1, chunks):
        backward(i, scales)
    push_step, back_step, self_step = products(CHUNK, nodes, True)
    loop(groups, push_step)
    loop(chunks, back_step)
    loop(xs, self_step)

    each(zs, lambda k: push_gz(k).wait())
    linked = r.zsend_g[z]
    for k in range(zs - 1):
        linked = linked + r.zsend_g_in[k]
    r.own_sum[y] = linked
    spread = col_sum(r.own_sum, 2)
    each(ys, lambda k: spread(k).start())

    each(ys, lambda k: sum_b(k).wait())
    backward(0, by_row(r.sums_b))
    push_step, back_step, self_step = products(0, CHUNK, False)

    def push2(pg, k):
        return copy(r.push2_low.at[pg], r.push2_in.at[k - 1], r.sems_g, 3, k - 1, g_peer(k)[1])

    def push2_to(k):
        pg = g_peer(k)[0]
        push_step(pg)
        r.push2_low[pg] = r.push2[pg, 0:hubs_z].astype(BF16)
        push2(pg, k).start()

    each(groups, push2_to)
    push_step(g)

    def swap(q):
        return copy(r.part.at[1 - c, q], r.part_in.at[q], r.sems_x, 2, q, partner)

    def quarters(body):
        each(xs, lambda k: body(x_peer(k)[0]))
        body(x)

    def self_quarter(q):
        self_step(q)

        @pl.when(c == 1)
        def _():
            swap(q).start()

    quarters(self_quarter)
    loop(chunks, back_step)
    r.back_low[...] = r.back[...].astype(BF16)

    def neigh_quarter(q):
        cols = pl.ds(pl.multiple_of(q * q_rows, q_rows), q_rows)
        r.part[1, q] = lax.dot_general(
            r.feat[:, cols], r.back_low[...], TALL, preferred_element_type=F32
        )

    quarters(neigh_quarter)

    def send_x(k):
        px, target = x_peer(k)
        return copy(r.xsend.at[px], r.xsend_in.at[k - 1], r.sems_x, 0, k - 1, target)

    def open_x():
        def step(k):
            px = x_peer(k)[0]
            swap(px).wait_recv()
            r.xsend[px] = (r.part[c, px] + r.part_in[px]).astype(BF16)
            send_x(k).start()

        each(xs, step)
        swap(x).wait_recv()
        r.total[...] = r.part[c, x] + r.part_in[x]

    @pl.when(c == 0)
    def _():
        open_x()

    each(zs, lambda k: gather_f(k).wait())
    hub_feat = r.hub_feat[...].astype(F32)
    for i in range(2):
        block = hub_feat[:, i * HUB_DEV : (i + 1) * HUB_DEV].reshape(hubs_z, half).astype(BF16)
        r.tall[0:hubs_z, i * half : (i + 1) * half] = block
        r.tall[hubs_z : 2 * hubs_z, i * half : (i + 1) * half] = block
    each(ys, lambda k: spread(k).wait())
    linked = jnp.concatenate([r.own_sum[i] for i in range(ys)], axis=1)
    linked_high = linked.astype(BF16).astype(F32)
    r.tall[2 * hubs_z :, :] = jnp.concatenate([linked_high, linked - linked_high], axis=0).astype(BF16)
    own_scaled = r.scaled[0:16, :].astype(F32)[0:HUB_DEV]
    each(groups, lambda k: push2(g_peer(k)[0], k).wait())
    summed = r.push2[g, 0:hubs_z]
    for k in range(groups - 1):
        summed = summed + r.push2_in[k].astype(F32)
    high = summed.astype(BF16).astype(F32)
    flat = jnp.concatenate([high, summed - high, own_scaled, own_scaled], axis=0).astype(BF16)

    def hub_quarter(q):
        cols = pl.ds(pl.multiple_of(q * q_rows, q_rows), q_rows)
        r.part[1, q] = r.part[1, q] + lax.dot_general(
            r.tall[:, cols], flat, TALL, preferred_element_type=F32
        )

        @pl.when(c == 0)
        def _():
            swap(q).start()

    quarters(hub_quarter)

    @pl.when(c == 1)
    def _():
        open_x()

    each(xs, lambda k: send_x(k).wait())
    reduced = r.total[...]
    for k in range(xs - 1):
        reduced = reduced + r.xsend_in[k].astype(F32)
    r.quarter[...] = reduced.reshape(owners, s.o_rows, width)
    r.zq[...] = reduced.astype(BF16).reshape(owners, s.o_rows, width)

    def owns(pz):
        return lax.rem(pz, 3) != 2

    def rank(pz):
        return (pz // 3) * 2 + lax.rem(pz, 3)

    def send_q(k):
        pz, target = z_peer(k)
        return copy(r.zq.at[rank(pz)], r.zq_in.at[k - 1], r.sems_z, 4, k - 1, target)

    def wait_q(k):
        return copy(r.zq.at[0], r.zq_in.at[k - 1], r.sems_z, 4, k - 1, z_peer(k)[1])

    def send_f(k):
        mine = r.final.at[c, x, rank(z)]
        return copy(mine, mine, r.sems_z, 5, k - 1, z_peer(k)[1])

    def wait_f(k):
        piece = r.final.at[c, x, 0]
        return copy(piece, piece, r.sems_z, 5, k - 1, z_peer(k)[1])

    def send_xf(piece, k):
        mine = r.final.at[c, x, piece]
        return copy(mine, mine, r.sems_f, k - 1, piece, x_peer(k)[1])

    def start_q(k):
        @pl.when(owns(z_peer(k)[0]))
        def _():
            send_q(k).start()

    each(zs, start_q)

    @pl.when(owns(z))
    def _():
        mine = r.quarter[rank(z)]
        each_near(zs, lambda k: wait_q(k).wait_recv())
        for k in range(zs - 1):
            mine = mine + r.zq_in[k].astype(F32)
        r.final[c, x, rank(z)] = mine.astype(BF16)
        each(zs, lambda k: send_f(k).start())
        each(xs, lambda k: send_xf(rank(z), k).start())

    def arrive(k):
        source = lax.rem(z + zs - k, zs)

        @pl.when(owns(source))
        def _():
            wait_f(k).wait_recv()
            each(xs, lambda j: send_xf(rank(source), j).start())

    each_near(zs, arrive)

    def hand_over(k, px):
        piece = r.final.at[c, px]
        return copy(piece, piece, r.sems_x, 1, k, partner)

    hand_over(0, x).start()

    def pass_on(k):
        loop(owners, lambda piece: send_xf(piece, k).wait_recv())
        hand_over(k, lax.rem(x + xs - k, xs)).start()

    each_near(xs, pass_on)

    def finish_q(k):
        @pl.when(owns(z_peer(k)[0]))
        def _():
            wait_q(k).wait_send()

    each(zs, finish_q)

    @pl.when(owns(z))
    def _():
        each(zs, lambda k: wait_f(k).wait_send())

    each(xs, lambda k: loop(owners, lambda piece: send_xf(piece, k).wait_send()))
    loop(xs, lambda q: swap(q).wait_send())
    loop(xs, lambda k: hand_over(k, 0).wait())
    grads[...] = r.final[...].reshape(CORES, s.depth, width)


def local(dims, features, w_self, w_neigh, local_nbr, hub_link, hub_used, cotangent):
    nodes, depth = features.shape
    s = sizes(dims, nodes, depth, w_self.shape[1])
    scratch = scratch_of(s)
    output, grads = pl.pallas_call(
        functools.partial(kernel, s, tuple(scratch)),
        out_shape=(
            jax.ShapeDtypeStruct((nodes, s.width), BF16),
            jax.ShapeDtypeStruct((CORES, depth, s.width), BF16),
        ),
        in_specs=[pl.BlockSpec(memory_space=pl.ANY)] * 7,
        out_specs=(pl.BlockSpec(memory_space=pltpu.VMEM),) * 2,
        scratch_shapes=list(scratch.values()),
        compiler_params=pltpu.CompilerParams(
            collective_id=0, has_side_effects=True, vmem_limit_bytes=56 * 1024 * 1024
        ),
    )(features, w_self, w_neigh, local_nbr.T, hub_link.T, hub_used.T, cotangent)
    return output, grads[0].astype(F32), grads[1].astype(F32)


def solution(mesh):
    ys = mesh.shape["cols"]
    xs = X_CHIPS
    zs = mesh.shape["nodes"] // (xs * CORES)
    placed = (
        P("nodes", None),
        P(None, "cols"),
        P(None, "cols"),
        P("nodes", None),
        P("nodes", None),
        P("nodes", None),
        P("nodes", "cols"),
    )
    return jax.shard_map(
        functools.partial(local, (xs, zs, ys)),
        mesh=mesh,
        in_specs=placed,
        out_specs=(P("nodes", "cols"), P(None, "cols"), P(None, "cols")),
        check_vma=False,
    )
```

```python
import functools
import types

import jax
import jax.numpy as jnp
from jax import lax
from jax.experimental import pallas as pl
from jax.experimental.pallas import tpu as pltpu
from jax.sharding import PartitionSpec as P

HUB_DEV = 8
FAN = 8
CORES = 2
GROUP_ROWS = 128
CHUNK = 256
TILE = 32
EPSILON = 1e-05
X_CHIPS = 4

F32 = jnp.float32
BF16 = jnp.bfloat16
TALL = (((0,), (0,)), ((), ()))
WIDE = (((1,), (1,)), ((), ()))


def sizes(dims, nodes, depth, width):
    xs, zs, ys = dims
    s = types.SimpleNamespace(xs=xs, zs=zs, ys=ys, nodes=nodes, depth=depth, width=width)
    s.groups = xs * CORES
    s.hubs_z = zs * HUB_DEV
    s.owners = 2 * zs // 3
    s.q_rows = depth // xs
    s.o_rows = s.q_rows // s.owners
    s.link_cols = s.groups * GROUP_ROWS
    s.chunks = nodes // CHUNK
    return s


def scratch_of(s):
    vmem = pltpu.VMEM
    dma = pltpu.SemaphoreType.DMA
    w = s.width
    hub_k = 2 * s.hubs_z + 2 * HUB_DEV
    return {
        "feat": vmem((s.nodes, s.depth), BF16),
        "w_self": vmem((s.depth, w), BF16),
        "w_neigh": vmem((s.depth, w), BF16),
        "nbr": vmem((FAN, s.nodes), jnp.int32),
        "link": vmem((4, s.nodes), jnp.int32),
        "used": vmem((4, s.nodes), jnp.int32),
        "cot": vmem((s.nodes, w), BF16),
        "links": vmem((s.link_cols, s.nodes), BF16),
        "locals_": vmem((s.nodes, s.nodes), BF16),
        "proj_self": vmem((s.nodes, w), F32),
        "pushable": vmem((s.nodes, 2 * w), BF16),
        "hub_rows": vmem((s.groups, GROUP_ROWS, w), BF16),
        "near": vmem((s.nodes, w), F32),
        "degree": vmem((s.nodes, w), F32),
        "push": vmem((s.groups, s.hubs_z, 2 * w), F32),
        "push_p": vmem((s.groups, s.hubs_z, w), BF16),
        "push_p_in": vmem((s.groups - 1, s.hubs_z, w), BF16),
        "push_c": vmem((s.groups, 2 * HUB_DEV, GROUP_ROWS), BF16),
        "push_c_in": vmem((s.groups - 1, 2 * HUB_DEV, GROUP_ROWS), BF16),
        "push_g": vmem((s.groups, s.hubs_z, w), BF16),
        "push_g_in": vmem((s.groups - 1, s.hubs_z, w), BF16),
        "zsum_p": vmem((s.zs, HUB_DEV, w), F32),
        "zsend_p": vmem((s.zs, 2 * HUB_DEV, w), BF16),
        "zsend_p_in": vmem((s.zs - 1, 2 * HUB_DEV, w), BF16),
        "zsend_g": vmem((s.zs, HUB_DEV, w), F32),
        "zsend_g_in": vmem((s.zs - 1, HUB_DEV, w), F32),
        "own_p": vmem((s.zs, HUB_DEV, w), F32),
        "own_sum": vmem((s.ys, HUB_DEV, w), F32),
        "hub_feat": vmem((s.zs, 2 * HUB_DEV, s.depth // 2), BF16),
        "sums": vmem((s.ys, 2 * s.chunks, CHUNK), F32),
        "act": vmem((s.nodes, w), F32),
        "act_slope": vmem((s.nodes, w), F32),
        "cot_slope": vmem((s.nodes, w), F32),
        "lows": vmem((s.nodes, 2 * w), BF16),
        "scaled": vmem((s.nodes, w), BF16),
        "push2_low": vmem((s.groups, s.hubs_z, w), BF16),
        "push2_in": vmem((s.groups - 1, s.hubs_z, w), BF16),
        "tall": vmem((hub_k, s.depth), BF16),
        "part": vmem((CORES, s.xs, s.q_rows, w), F32),
        "part_in": vmem((s.xs, s.q_rows, w), F32),
        "total": vmem((s.q_rows, w), F32),
        "xsend": vmem((s.xs, s.q_rows, w), BF16),
        "xsend_in": vmem((s.xs - 1, s.q_rows, w), BF16),
        "quarter": vmem((s.owners, s.o_rows, w), F32),
        "zq": vmem((s.owners, s.o_rows, w), BF16),
        "zq_in": vmem((s.zs - 1, s.o_rows, w), BF16),
        "final": vmem((CORES, s.xs, s.owners, s.o_rows, w), BF16),
        "sems_z": dma((2, 6, s.zs - 1)),
        "sems_g": dma((2, 5, s.groups - 1)),
        "sems_y": dma((2, 2, s.ys - 1)),
        "sems_x": dma((2, 3, s.xs)),
        "sems_f": dma((2, s.xs - 1, s.owners)),
        "sems_l": dma((7,)),
    }


def kernel(s, names, feat_in, w_self_in, w_neigh_in, nbr_in, link_in, used_in, cot_in, out, grads, *refs):
    r = types.SimpleNamespace(**dict(zip(names, refs)))
    xs, zs, ys, width, nodes = s.xs, s.zs, s.ys, s.width, s.nodes
    groups, hubs_z, owners, q_rows = s.groups, s.hubs_z, s.owners, s.q_rows
    chunks = s.chunks
    me = lax.axis_index("nodes")
    y = lax.axis_index("cols")
    c = lax.rem(me, CORES)
    z = lax.rem(me // CORES, zs)
    x = me // (CORES * zs)
    g = x * CORES + c

    def node(px, pz, pc):
        return (px * zs + pz) * CORES + pc

    def copy(src, dst, sems, row, slot, target):
        return pltpu.make_async_remote_copy(
            src_ref=src,
            dst_ref=dst,
            send_sem=sems.at[0, row, slot],
            recv_sem=sems.at[1, row, slot],
            device_id=target,
            device_id_type=pl.DeviceIdType.MESH,
        )

    def loop(count, body):
        def step(i, carry):
            body(i)
            return carry

        lax.fori_loop(0, count, step, 0)

    def ranked(count, i):
        return count // 2 + (i // 2) * (1 - 2 * lax.rem(i, 2))

    def each(count, body):
        loop(count - 1, lambda i: body(ranked(count, i + 1)))

    def each_near(count, body):
        loop(count - 1, lambda i: body(ranked(count, count - 1 - i)))

    def z_peer(k):
        pz = lax.rem(z + k, zs)
        return pz, (node(x, pz, c), y)

    def g_peer(k):
        px = lax.rem(x + k // CORES, xs)
        pc = lax.rem(c + lax.rem(k, CORES), CORES)
        return px * CORES + pc, (node(px, z, pc), y)

    def y_peer(k):
        return me, lax.rem(y + k, ys)

    def x_peer(k):
        px = lax.rem(x + k, xs)
        return px, (node(px, z, c), y)

    partner = (node(x, z, 1 - c), y)

    barrier = pltpu.get_barrier_semaphore()

    def greet(target):
        pl.semaphore_signal(barrier, inc=1, device_id=target, device_id_type=pl.DeviceIdType.MESH)

    inputs = [
        pltpu.make_async_copy(src, dst, r.sems_l.at[i])
        for i, (src, dst) in enumerate(
            (
                (link_in, r.link),
                (used_in, r.used),
                (w_neigh_in, r.w_neigh),
                (feat_in, r.feat),
                (w_self_in, r.w_self),
                (nbr_in, r.nbr),
                (cot_in, r.cot),
            )
        )
    ]
    for item in inputs:
        item.start()
    each(zs, lambda k: greet(z_peer(k)[1]))
    each(ys, lambda k: greet(y_peer(k)))
    each(groups, lambda k: greet(g_peer(k)[1]))
    r.hub_rows[:, hubs_z:] = jnp.zeros((groups, GROUP_ROWS - hubs_z, width), BF16)

    def build(dest, base, count, picks):
        near_ids = (picks - base).astype(jnp.int16)
        ids = lax.broadcasted_iota(jnp.int16, (count, nodes), 0)
        acc = jnp.zeros((count, nodes), BF16)
        for k in range(picks.shape[0]):
            hit = ids == near_ids[k : k + 1, :]
            acc = acc + jnp.where(hit, jnp.bfloat16(1.0), jnp.bfloat16(0.0))
        dest[pl.ds(pl.multiple_of(base, GROUP_ROWS), count), :] = acc

    inputs[0].wait()
    inputs[1].wait()
    hub = r.link[...]
    place = lax.rem(hub, HUB_DEV)
    device = lax.div(hub, HUB_DEV)
    core = lax.rem(device, CORES)
    chip = lax.div(device, CORES)
    hub_x = jnp.zeros_like(chip)
    for i in range(1, xs):
        hub_x = hub_x + (chip >= i * zs).astype(jnp.int32)
    hub_z = chip - hub_x * zs
    column = (hub_x * CORES + core) * GROUP_ROWS + hub_z * HUB_DEV + place
    r.link[...] = jnp.where(r.used[...] > 0, column, -1)
    tiles = -(-hubs_z // TILE) * TILE

    def build_links(i):
        base = i * GROUP_ROWS
        build(r.links, base, tiles, r.link[...])
        if tiles < GROUP_ROWS:
            rest = GROUP_ROWS - tiles
            r.links[pl.ds(pl.multiple_of(base + tiles, TILE), rest), :] = jnp.zeros((rest, nodes), BF16)

    loop(groups, build_links)

    inputs[2].wait()
    inputs[3].wait()
    own_rows = r.feat[0:16, :]
    r.own_p[z] = jnp.dot(own_rows, r.w_neigh[...], preferred_element_type=F32)[0:HUB_DEV]

    def gather_z(k):
        mine = r.own_p.at[z]
        return copy(mine, mine, r.sems_z, 0, k - 1, z_peer(k)[1])

    def proj_step(i):
        rows = pl.ds(pl.multiple_of(i * CHUNK, CHUNK), CHUNK)
        r.pushable[rows, 0:width] = jnp.dot(
            r.feat[rows, :], r.w_neigh[...], preferred_element_type=F32
        ).astype(BF16)
        r.pushable[rows, width:] = r.feat[rows, pl.ds(pl.multiple_of(y * width, 128), width)]

    loop(chunks, proj_step)

    def push_p(pg, k):
        target = g_peer(k)[1]
        return copy(r.push_p.at[pg], r.push_p_in.at[k - 1], r.sems_g, 0, k - 1, target)

    def push_g(pg, k):
        target = g_peer(k)[1]
        return copy(r.push_g.at[pg], r.push_g_in.at[k - 1], r.sems_g, 1, k - 1, target)

    def push_c(pg, k):
        target = g_peer(k)[1]
        return copy(r.push_c.at[pg], r.push_c_in.at[k - 1], r.sems_g, 4, k - 1, target)

    def push_rows(pg):
        rows = r.links[pl.ds(pl.multiple_of(pg * GROUP_ROWS, GROUP_ROWS), GROUP_ROWS), :]
        both = jnp.dot(rows, r.pushable[...], preferred_element_type=F32)[0:hubs_z]
        r.push[pg] = both
        r.push_p[pg] = both[:, :width].astype(BF16)
        r.push_g[pg] = both[:, width:].astype(BF16)

    loop(groups, push_rows)
    pl.semaphore_wait(barrier, zs + groups + ys - 3)
    each(zs, lambda k: gather_z(k).start())
    each(groups, lambda k: push_p(g_peer(k)[0], k).start())

    def split_count(count):
        high = count.astype(BF16).astype(F32)
        return jnp.concatenate([high, count - high], axis=0).astype(BF16)

    count = lax.dot_general(
        jnp.ones((HUB_DEV, nodes), BF16), r.links[...], WIDE, preferred_element_type=F32
    )
    for i in range(groups):
        r.push_c[i] = split_count(count[:, i * GROUP_ROWS : (i + 1) * GROUP_ROWS])
    each(groups, lambda k: push_c(g_peer(k)[0], k).start())
    each(groups, lambda k: push_g(g_peer(k)[0], k).start())

    inputs[5].wait()
    loop(nodes // GROUP_ROWS, lambda i: build(r.locals_, i * GROUP_ROWS, GROUP_ROWS, r.nbr[...]))

    each(groups, lambda k: push_p(g_peer(k)[0], k).wait())
    each(groups, lambda k: push_c(g_peer(k)[0], k).wait())
    summed = r.push[g, :, 0:width]
    counts = r.push_c[g].astype(F32)
    for k in range(groups - 1):
        summed = summed + r.push_p_in[k].astype(F32)
        counts = counts + r.push_c_in[k].astype(F32)
    counts = counts[0:HUB_DEV] + counts[HUB_DEV:]
    high = counts.astype(BF16).astype(F32)
    part_row = lax.broadcasted_iota(jnp.int32, counts.shape, 0)
    parts = jnp.where(part_row == 0, high, jnp.where(part_row == 1, counts - high, 0.0))
    r.zsum_p[...] = summed.reshape(zs, HUB_DEV, width)
    for i in range(zs):
        rows = summed[i * HUB_DEV : (i + 1) * HUB_DEV]
        r.zsend_p[i] = jnp.concatenate([rows, parts], axis=0).astype(BF16)

    def push_pz(k):
        pz, target = z_peer(k)
        return copy(r.zsend_p.at[pz], r.zsend_p_in.at[k - 1], r.sems_z, 1, k - 1, target)

    each(zs, lambda k: push_pz(k).start())

    inputs[4].wait()

    def near_step(i):
        rows = pl.ds(pl.multiple_of(i * CHUNK, CHUNK), CHUNK)
        r.proj_self[rows, :] = jnp.dot(r.feat[rows, :], r.w_self[...], preferred_element_type=F32)
        r.near[rows, :] = lax.dot_general(
            r.locals_[:, rows], r.pushable[:, 0:width], TALL, preferred_element_type=F32
        )
        r.degree[rows, :] = FAN + lax.dot_general(
            r.links[:, rows], jnp.ones((s.link_cols, width), BF16), TALL, preferred_element_type=F32
        )

    loop(chunks, near_step)

    each(zs, lambda k: gather_z(k).wait())
    r.hub_rows[g, 0:hubs_z] = r.own_p[...].reshape(hubs_z, width).astype(BF16)

    def gather_g(k):
        mine = r.hub_rows.at[g, pl.ds(0, hubs_z)]
        return copy(mine, mine, r.sems_g, 2, k - 1, g_peer(k)[1])

    each(groups, lambda k: gather_g(k).start())

    each(groups, lambda k: push_g(g_peer(k)[0], k).wait())
    summed = r.push[g, :, width:]
    for k in range(groups - 1):
        summed = summed + r.push_g_in[k].astype(F32)
    r.zsend_g[...] = summed.reshape(zs, HUB_DEV, width)

    def push_gz(k):
        pz, target = z_peer(k)
        return copy(r.zsend_g.at[pz], r.zsend_g_in.at[k - 1], r.sems_z, 2, k - 1, target)

    each(zs, lambda k: push_gz(k).start())

    each(groups, lambda k: gather_g(k).wait())
    inputs[6].wait()

    def pull(i):
        rows = slice(i * CHUNK, (i + 1) * CHUNK)
        r.near[rows, :] = r.near[rows, :] + lax.dot_general(
            r.links[:, rows],
            r.hub_rows[...].reshape(s.link_cols, width),
            TALL,
            preferred_element_type=F32,
        )

    def activate(i):
        rows = slice(i * CHUNK, (i + 1) * CHUNK)
        picks = lax.broadcasted_iota(jnp.int32, (2 * chunks, width), 0)
        per_degree = 1.0 / r.degree[rows, :]
        pre = r.proj_self[rows, :] + r.near[rows, :] * per_degree
        sig = jax.nn.sigmoid(pre)
        act = pre * sig
        slope = sig * (1.0 + pre * (1.0 - sig))
        cot = r.cot[rows, :].astype(F32)
        r.degree[rows, :] = per_degree
        r.act[rows, :] = act
        r.act_slope[rows, :] = act * slope
        r.cot_slope[rows, :] = cot * slope
        sums = jnp.zeros((2 * chunks, CHUNK), F32)
        for at, value in ((i, act * act), (chunks + i, act * cot)):
            sums = sums + lax.dot_general(
                jnp.where(picks == at, 1.0, 0.0),
                value,
                WIDE,
                preferred_element_type=F32,
                precision=lax.Precision.HIGHEST,
            )
        return sums

    sums = jnp.zeros((2 * chunks, CHUNK), F32)
    for i in range(1, chunks):
        pull(i)
        sums = sums + activate(i)
    pull(0)

    each(zs, lambda k: push_pz(k).wait())
    inflow = r.zsum_p[z]
    counts = r.zsend_p[z].astype(F32)[HUB_DEV:]
    for k in range(zs - 1):
        block = r.zsend_p_in[k].astype(F32)
        inflow = inflow + block[0:HUB_DEV]
        counts = counts + block[HUB_DEV:]
    counts = jnp.sum(counts, axis=0, keepdims=True)
    lane = lax.broadcasted_iota(jnp.int32, (HUB_DEV, GROUP_ROWS), 1)
    sub = lax.broadcasted_iota(jnp.int32, (HUB_DEV, GROUP_ROWS), 0)
    count_in = jnp.sum(jnp.where(lane == sub + z * HUB_DEV, counts, 0.0), axis=1, keepdims=True)
    r.near[0:HUB_DEV, :] = r.near[0:HUB_DEV, :] + inflow
    r.degree[0:HUB_DEV, :] = r.degree[0:HUB_DEV, :] + count_in
    r.sums[y] = sums + activate(0)

    def col_sum(buf, row):
        return lambda k: copy(buf.at[y], buf.at[y], r.sems_y, row, k - 1, y_peer(k))

    col_sums = col_sum(r.sums, 0)
    each(ys, lambda k: col_sums(k).start())

    own_f32 = r.feat[0:16, :].astype(F32)[0:HUB_DEV]
    half = s.depth // 2
    r.hub_feat[z] = jnp.concatenate([own_f32[:, :half], own_f32[:, half:]], axis=0).astype(BF16)

    def gather_f(k):
        mine = r.hub_feat.at[z]
        return copy(mine, mine, r.sems_z, 3, k - 1, z_peer(k)[1])

    each(zs, lambda k: gather_f(k).start())

    each(zs, lambda k: push_gz(k).wait())
    linked = r.zsend_g[z]
    for k in range(zs - 1):
        linked = linked + r.zsend_g_in[k]
    r.own_sum[y] = linked
    spread = col_sum(r.own_sum, 1)
    each(ys, lambda k: spread(k).start())

    each(ys, lambda k: col_sums(k).wait())
    sums = r.sums[0]
    for i in range(1, ys):
        sums = sums + r.sums[i]
    inv_scale = 1.0 / jnp.sqrt(sums[0:chunks] / s.depth + EPSILON)
    inner = sums[chunks:] * inv_scale / s.depth
    scales = jnp.transpose(jnp.concatenate([inv_scale, inv_scale * inv_scale * inner], axis=0))
    for i in range(chunks):
        rows = slice(i * CHUNK, (i + 1) * CHUNK)
        grad = (
            r.cot_slope[rows, :] * scales[:, i : i + 1]
            - r.act_slope[rows, :] * scales[:, chunks + i : chunks + i + 1]
        )
        r.lows[rows, 0:width] = grad.astype(BF16)
        r.scaled[rows, :] = (grad * r.degree[rows, :]).astype(BF16)

    def push2(pg, k):
        return copy(r.push2_low.at[pg], r.push2_in.at[k - 1], r.sems_g, 3, k - 1, g_peer(k)[1])

    def push2_rows(pg):
        rows = pl.ds(pl.multiple_of(pg * GROUP_ROWS, GROUP_ROWS), GROUP_ROWS)
        value = jnp.dot(r.links[rows, :], r.scaled[...], preferred_element_type=F32)
        return value[0:hubs_z]

    def push2_to(k):
        pg = g_peer(k)[0]
        r.push2_low[pg] = push2_rows(pg).astype(BF16)
        push2(pg, k).start()

    each(groups, push2_to)
    own_push2 = push2_rows(g)

    def back_step(i):
        rows = pl.ds(pl.multiple_of(i * CHUNK, CHUNK), CHUNK)
        r.lows[rows, width:] = jnp.dot(
            r.locals_[rows, :], r.scaled[...], preferred_element_type=F32
        ).astype(BF16)

    loop(chunks, back_step)

    def swap(q):
        return copy(r.part.at[1 - c, q], r.part_in.at[q], r.sems_x, 2, q, partner)

    def quarters(body):
        each(xs, lambda k: body(x_peer(k)[0]))
        body(x)

    def grad_quarter(q):
        cols = pl.ds(pl.multiple_of(q * q_rows, q_rows), q_rows)
        both = lax.dot_general(r.feat[:, cols], r.lows[...], TALL, preferred_element_type=F32)
        r.part[0, q] = both[:, :width]
        r.part[1, q] = both[:, width:]

        @pl.when(c == 1)
        def _():
            swap(q).start()

    quarters(grad_quarter)

    def send_x(k):
        px, target = x_peer(k)
        return copy(r.xsend.at[px], r.xsend_in.at[k - 1], r.sems_x, 0, k - 1, target)

    def open_x():
        def step(k):
            px = x_peer(k)[0]
            swap(px).wait_recv()
            r.xsend[px] = (r.part[c, px] + r.part_in[px]).astype(BF16)
            send_x(k).start()

        each(xs, step)
        swap(x).wait_recv()
        r.total[...] = r.part[c, x] + r.part_in[x]

    @pl.when(c == 0)
    def _():
        open_x()

    each(zs, lambda k: gather_f(k).wait())
    hub_feat = r.hub_feat[...].astype(F32)
    for i in range(2):
        block = hub_feat[:, i * HUB_DEV : (i + 1) * HUB_DEV].reshape(hubs_z, half).astype(BF16)
        r.tall[0:hubs_z, i * half : (i + 1) * half] = block
        r.tall[hubs_z : 2 * hubs_z, i * half : (i + 1) * half] = block
    each(ys, lambda k: spread(k).wait())
    linked = jnp.concatenate([r.own_sum[i] for i in range(ys)], axis=1)
    linked_high = linked.astype(BF16).astype(F32)
    r.tall[2 * hubs_z :, :] = jnp.concatenate([linked_high, linked - linked_high], axis=0).astype(BF16)
    own_scaled = r.scaled[0:16, :].astype(F32)[0:HUB_DEV]
    each(groups, lambda k: push2(g_peer(k)[0], k).wait())
    summed = own_push2
    for k in range(groups - 1):
        summed = summed + r.push2_in[k].astype(F32)
    high = summed.astype(BF16).astype(F32)
    flat = jnp.concatenate([high, summed - high, own_scaled, own_scaled], axis=0).astype(BF16)

    def hub_quarter(q):
        cols = pl.ds(pl.multiple_of(q * q_rows, q_rows), q_rows)
        r.part[1, q] = r.part[1, q] + lax.dot_general(
            r.tall[:, cols], flat, TALL, preferred_element_type=F32
        )

        @pl.when(c == 0)
        def _():
            swap(q).start()

    quarters(hub_quarter)

    @pl.when(c == 1)
    def _():
        open_x()

    for i in range(chunks):
        rows = slice(i * CHUNK, (i + 1) * CHUNK)
        out[rows, :] = (r.act[rows, :] * scales[:, i : i + 1]).astype(BF16)

    each(xs, lambda k: send_x(k).wait())
    reduced = r.total[...]
    for k in range(xs - 1):
        reduced = reduced + r.xsend_in[k].astype(F32)
    r.quarter[...] = reduced.reshape(owners, s.o_rows, width)
    r.zq[...] = reduced.astype(BF16).reshape(owners, s.o_rows, width)

    def owns(pz):
        return lax.rem(pz, 3) != 2

    def rank(pz):
        return (pz // 3) * 2 + lax.rem(pz, 3)

    def send_q(k):
        pz, target = z_peer(k)
        return copy(r.zq.at[rank(pz)], r.zq_in.at[k - 1], r.sems_z, 4, k - 1, target)

    def wait_q(k):
        return copy(r.zq.at[0], r.zq_in.at[k - 1], r.sems_z, 4, k - 1, z_peer(k)[1])

    def send_f(k):
        mine = r.final.at[c, x, rank(z)]
        return copy(mine, mine, r.sems_z, 5, k - 1, z_peer(k)[1])

    def wait_f(k):
        piece = r.final.at[c, x, 0]
        return copy(piece, piece, r.sems_z, 5, k - 1, z_peer(k)[1])

    def send_xf(piece, k):
        mine = r.final.at[c, x, piece]
        return copy(mine, mine, r.sems_f, k - 1, piece, x_peer(k)[1])

    def start_q(k):
        @pl.when(owns(z_peer(k)[0]))
        def _():
            send_q(k).start()

    each(zs, start_q)

    @pl.when(owns(z))
    def _():
        mine = r.quarter[rank(z)]
        each_near(zs, lambda k: wait_q(k).wait_recv())
        for k in range(zs - 1):
            mine = mine + r.zq_in[k].astype(F32)
        r.final[c, x, rank(z)] = mine.astype(BF16)
        each(zs, lambda k: send_f(k).start())
        each(xs, lambda k: send_xf(rank(z), k).start())

    def arrive(k):
        source = lax.rem(z + zs - k, zs)

        @pl.when(owns(source))
        def _():
            wait_f(k).wait_recv()
            each(xs, lambda j: send_xf(rank(source), j).start())

    each_near(zs, arrive)

    def hand_over(k, px):
        piece = r.final.at[c, px]
        return copy(piece, piece, r.sems_x, 1, k, partner)

    hand_over(0, x).start()

    def pass_on(k):
        loop(owners, lambda piece: send_xf(piece, k).wait_recv())
        hand_over(k, lax.rem(x + xs - k, xs)).start()

    each_near(xs, pass_on)

    def finish_q(k):
        @pl.when(owns(z_peer(k)[0]))
        def _():
            wait_q(k).wait_send()

    each(zs, finish_q)

    @pl.when(owns(z))
    def _():
        each(zs, lambda k: wait_f(k).wait_send())

    each(xs, lambda k: loop(owners, lambda piece: send_xf(piece, k).wait_send()))
    loop(xs, lambda q: swap(q).wait_send())
    loop(xs, lambda k: hand_over(k, 0).wait())
    grads[...] = r.final[...].reshape(CORES, s.depth, width)


def finish(output_in, grads_in, output_out, self_out, neigh_out, rows, low, high, sems):
    count, half = low.shape[0], low.shape[1]
    loads = []
    stores = []
    for i in range(count):
        part = pl.ds(i % 2 * half, half)
        target = (self_out, neigh_out)[i // 2]
        loads.append(pltpu.make_async_copy(grads_in.at[i // 2, part], low.at[i], sems.at[0, i]))
        stores.append(pltpu.make_async_copy(high.at[i], target.at[part], sems.at[1, i]))
    loads.append(pltpu.make_async_copy(output_in, rows, sems.at[0, count]))
    stores.append(pltpu.make_async_copy(rows, output_out, sems.at[1, count]))
    for load in loads:
        load.start()
    for i in range(count):
        loads[i].wait()
        high[i] = low[i].astype(F32)
        stores[i].start()
    loads[count].wait()
    stores[count].start()
    for store in stores:
        store.wait()


def local(dims, features, w_self, w_neigh, local_nbr, hub_link, hub_used, cotangent):
    nodes, depth = features.shape
    s = sizes(dims, nodes, depth, w_self.shape[1])
    scratch = scratch_of(s)
    output, grads = pl.pallas_call(
        functools.partial(kernel, s, tuple(scratch)),
        out_shape=(
            jax.ShapeDtypeStruct((nodes, s.width), BF16),
            jax.ShapeDtypeStruct((CORES, depth, s.width), BF16),
        ),
        in_specs=[pl.BlockSpec(memory_space=pl.ANY)] * 7,
        out_specs=(pl.BlockSpec(memory_space=pltpu.VMEM),) * 2,
        scratch_shapes=list(scratch.values()),
        compiler_params=pltpu.CompilerParams(
            collective_id=0, has_side_effects=True, vmem_limit_bytes=56 * 1024 * 1024
        ),
    )(features, w_self, w_neigh, local_nbr.T, hub_link.T, hub_used.T, cotangent)
    grad = jax.ShapeDtypeStruct((depth, s.width), F32)
    return pl.pallas_call(
        finish,
        out_shape=(jax.ShapeDtypeStruct((nodes, s.width), BF16), grad, grad),
        in_specs=[pl.BlockSpec(memory_space=pl.ANY)] * 2,
        out_specs=(pl.BlockSpec(memory_space=pl.ANY),) * 3,
        scratch_shapes=[
            pltpu.VMEM((nodes, s.width), BF16),
            pltpu.VMEM((2 * CORES, depth // 2, s.width), BF16),
            pltpu.VMEM((2 * CORES, depth // 2, s.width), F32),
            pltpu.SemaphoreType.DMA((2, 2 * CORES + 1)),
        ],
    )(output, grads)


def solution(mesh):
    ys = mesh.shape["cols"]
    xs = X_CHIPS
    zs = mesh.shape["nodes"] // (xs * CORES)
    placed = (
        P("nodes", None),
        P(None, "cols"),
        P(None, "cols"),
        P("nodes", None),
        P("nodes", None),
        P("nodes", None),
        P("nodes", "cols"),
    )
    return jax.shard_map(
        functools.partial(local, (xs, zs, ys)),
        mesh=mesh,
        in_specs=placed,
        out_specs=(P("nodes", "cols"), P(None, "cols"), P(None, "cols")),
        check_vma=False,
    )
```

```python
import functools
import types

import jax
import jax.numpy as jnp
from jax import lax
from jax.experimental import pallas as pl
from jax.experimental.pallas import tpu as pltpu
from jax.sharding import PartitionSpec as P

HUB_DEV = 8
FAN = 8
CORES = 2
GROUP_ROWS = 128
CHUNK = 256
TILE = 32
EPSILON = 1e-05
X_CHIPS = 4

F32 = jnp.float32
BF16 = jnp.bfloat16
TALL = (((0,), (0,)), ((), ()))
WIDE = (((1,), (1,)), ((), ()))


def sizes(dims, nodes, depth, width):
    xs, zs, ys = dims
    s = types.SimpleNamespace(xs=xs, zs=zs, ys=ys, nodes=nodes, depth=depth, width=width)
    s.groups = xs * CORES
    s.hubs_z = zs * HUB_DEV
    s.owners = 2 * zs // 3
    s.q_rows = depth // xs
    s.o_rows = s.q_rows // s.owners
    s.link_cols = s.groups * GROUP_ROWS
    s.chunks = nodes // CHUNK
    return s


def scratch_of(s):
    vmem = pltpu.VMEM
    dma = pltpu.SemaphoreType.DMA
    w = s.width
    hub_k = 2 * s.hubs_z + 2 * HUB_DEV
    return {
        "feat": vmem((s.nodes, s.depth), BF16),
        "w_self": vmem((s.depth, w), BF16),
        "w_neigh": vmem((s.depth, w), BF16),
        "nbr": vmem((FAN, s.nodes), jnp.int32),
        "link": vmem((4, s.nodes), jnp.int32),
        "used": vmem((4, s.nodes), jnp.int32),
        "cot": vmem((s.nodes, w), BF16),
        "links": vmem((s.link_cols, s.nodes), BF16),
        "locals_": vmem((s.nodes, s.nodes), BF16),
        "proj_self": vmem((s.nodes, w), F32),
        "pushable": vmem((s.nodes, 2 * w), BF16),
        "hub_rows": vmem((s.groups, GROUP_ROWS, w), BF16),
        "near": vmem((s.nodes, w), F32),
        "degree": vmem((s.nodes, w), F32),
        "push": vmem((s.groups, s.hubs_z, 2 * w), F32),
        "push_p": vmem((s.groups, s.hubs_z, w), BF16),
        "push_p_in": vmem((s.groups - 1, s.hubs_z, w), BF16),
        "push_c": vmem((s.groups, 2 * HUB_DEV, GROUP_ROWS), BF16),
        "push_c_in": vmem((s.groups - 1, 2 * HUB_DEV, GROUP_ROWS), BF16),
        "push_g": vmem((s.groups, s.hubs_z, w), BF16),
        "push_g_in": vmem((s.groups - 1, s.hubs_z, w), BF16),
        "zsum_p": vmem((s.zs, HUB_DEV, w), F32),
        "zsend_p": vmem((s.zs, 2 * HUB_DEV, w), BF16),
        "zsend_p_in": vmem((s.zs - 1, 2 * HUB_DEV, w), BF16),
        "zsend_g": vmem((s.zs, HUB_DEV, w), F32),
        "zsend_g_in": vmem((s.zs - 1, HUB_DEV, w), F32),
        "own_p": vmem((s.zs, HUB_DEV, w), F32),
        "own_sum": vmem((s.ys, HUB_DEV, w), F32),
        "hub_feat": vmem((s.zs, 2 * HUB_DEV, s.depth // 2), BF16),
        "sums": vmem((s.ys, 2 * s.chunks, CHUNK), F32),
        "act": vmem((s.nodes, w), F32),
        "act_slope": vmem((s.nodes, w), F32),
        "cot_slope": vmem((s.nodes, w), F32),
        "lows": vmem((s.nodes, 2 * w), BF16),
        "scaled": vmem((s.nodes, w), BF16),
        "push2_low": vmem((s.groups, s.hubs_z, w), BF16),
        "push2_in": vmem((s.groups - 1, s.hubs_z, w), BF16),
        "tall": vmem((hub_k, s.depth), BF16),
        "part": vmem((CORES, s.xs, s.q_rows, w), F32),
        "part_in": vmem((s.xs, s.q_rows, w), F32),
        "total": vmem((s.q_rows, w), F32),
        "xsend": vmem((s.xs, s.q_rows, w), BF16),
        "xsend_in": vmem((s.xs - 1, s.q_rows, w), BF16),
        "quarter": vmem((s.owners, s.o_rows, w), F32),
        "zq": vmem((s.owners, s.o_rows, w), BF16),
        "zq_in": vmem((s.zs - 1, s.o_rows, w), BF16),
        "final": vmem((CORES, s.xs, s.owners, s.o_rows, w), BF16),
        "sems_z": dma((2, 6, s.zs - 1)),
        "sems_g": dma((2, 5, s.groups - 1)),
        "sems_y": dma((2, 2, s.ys - 1)),
        "sems_x": dma((2, 3, s.xs)),
        "sems_f": dma((2, s.xs - 1, s.owners)),
        "output": vmem((s.nodes, w), BF16),
        "sems_l": dma((8,)),
        "sems_o": dma((CORES, s.xs)),
    }


def kernel(s, names, feat_in, w_self_in, w_neigh_in, nbr_in, link_in, used_in, cot_in, out, grads, *refs):
    r = types.SimpleNamespace(**dict(zip(names, refs)))
    xs, zs, ys, width, nodes = s.xs, s.zs, s.ys, s.width, s.nodes
    groups, hubs_z, owners, q_rows = s.groups, s.hubs_z, s.owners, s.q_rows
    chunks = s.chunks
    me = lax.axis_index("nodes")
    y = lax.axis_index("cols")
    c = lax.rem(me, CORES)
    z = lax.rem(me // CORES, zs)
    x = me // (CORES * zs)
    g = x * CORES + c

    def node(px, pz, pc):
        return (px * zs + pz) * CORES + pc

    def copy(src, dst, sems, row, slot, target):
        return pltpu.make_async_remote_copy(
            src_ref=src,
            dst_ref=dst,
            send_sem=sems.at[0, row, slot],
            recv_sem=sems.at[1, row, slot],
            device_id=target,
            device_id_type=pl.DeviceIdType.MESH,
        )

    def loop(count, body):
        def step(i, carry):
            body(i)
            return carry

        lax.fori_loop(0, count, step, 0)

    def ranked(count, i):
        return count // 2 + (i // 2) * (1 - 2 * lax.rem(i, 2))

    def each(count, body):
        loop(count - 1, lambda i: body(ranked(count, i + 1)))

    def each_near(count, body):
        loop(count - 1, lambda i: body(ranked(count, count - 1 - i)))

    def z_peer(k):
        pz = lax.rem(z + k, zs)
        return pz, (node(x, pz, c), y)

    def g_peer(k):
        px = lax.rem(x + k // CORES, xs)
        pc = lax.rem(c + lax.rem(k, CORES), CORES)
        return px * CORES + pc, (node(px, z, pc), y)

    def y_peer(k):
        return me, lax.rem(y + k, ys)

    def x_peer(k):
        px = lax.rem(x + k, xs)
        return px, (node(px, z, c), y)

    partner = (node(x, z, 1 - c), y)

    barrier = pltpu.get_barrier_semaphore()

    def greet(target):
        pl.semaphore_signal(barrier, inc=1, device_id=target, device_id_type=pl.DeviceIdType.MESH)

    inputs = [
        pltpu.make_async_copy(src, dst, r.sems_l.at[i])
        for i, (src, dst) in enumerate(
            (
                (link_in, r.link),
                (used_in, r.used),
                (w_neigh_in, r.w_neigh),
                (feat_in, r.feat),
                (w_self_in, r.w_self),
                (nbr_in, r.nbr),
                (cot_in, r.cot),
            )
        )
    ]
    for item in inputs:
        item.start()
    each(zs, lambda k: greet(z_peer(k)[1]))
    each(ys, lambda k: greet(y_peer(k)))
    each(groups, lambda k: greet(g_peer(k)[1]))
    r.hub_rows[:, hubs_z:] = jnp.zeros((groups, GROUP_ROWS - hubs_z, width), BF16)

    def build(dest, base, count, picks):
        near_ids = (picks - base).astype(jnp.int16)
        ids = lax.broadcasted_iota(jnp.int16, (count, nodes), 0)
        acc = jnp.zeros((count, nodes), BF16)
        for k in range(picks.shape[0]):
            hit = ids == near_ids[k : k + 1, :]
            acc = acc + jnp.where(hit, jnp.bfloat16(1.0), jnp.bfloat16(0.0))
        dest[pl.ds(pl.multiple_of(base, GROUP_ROWS), count), :] = acc

    inputs[0].wait()
    inputs[1].wait()
    hub = r.link[...]
    place = lax.rem(hub, HUB_DEV)
    device = lax.div(hub, HUB_DEV)
    core = lax.rem(device, CORES)
    chip = lax.div(device, CORES)
    hub_x = jnp.zeros_like(chip)
    for i in range(1, xs):
        hub_x = hub_x + (chip >= i * zs).astype(jnp.int32)
    hub_z = chip - hub_x * zs
    column = (hub_x * CORES + core) * GROUP_ROWS + hub_z * HUB_DEV + place
    r.link[...] = jnp.where(r.used[...] > 0, column, -1)
    tiles = -(-hubs_z // TILE) * TILE

    def build_links(i):
        base = i * GROUP_ROWS
        build(r.links, base, tiles, r.link[...])
        if tiles < GROUP_ROWS:
            rest = GROUP_ROWS - tiles
            r.links[pl.ds(pl.multiple_of(base + tiles, TILE), rest), :] = jnp.zeros((rest, nodes), BF16)

    loop(groups, build_links)

    inputs[2].wait()
    inputs[3].wait()
    own_rows = r.feat[0:16, :]
    r.own_p[z] = jnp.dot(own_rows, r.w_neigh[...], preferred_element_type=F32)[0:HUB_DEV]

    def gather_z(k):
        mine = r.own_p.at[z]
        return copy(mine, mine, r.sems_z, 0, k - 1, z_peer(k)[1])

    def proj_step(i):
        rows = pl.ds(pl.multiple_of(i * CHUNK, CHUNK), CHUNK)
        r.pushable[rows, 0:width] = jnp.dot(
            r.feat[rows, :], r.w_neigh[...], preferred_element_type=F32
        ).astype(BF16)
        r.pushable[rows, width:] = r.feat[rows, pl.ds(pl.multiple_of(y * width, 128), width)]

    loop(chunks, proj_step)

    def push_p(pg, k):
        target = g_peer(k)[1]
        return copy(r.push_p.at[pg], r.push_p_in.at[k - 1], r.sems_g, 0, k - 1, target)

    def push_g(pg, k):
        target = g_peer(k)[1]
        return copy(r.push_g.at[pg], r.push_g_in.at[k - 1], r.sems_g, 1, k - 1, target)

    def push_c(pg, k):
        target = g_peer(k)[1]
        return copy(r.push_c.at[pg], r.push_c_in.at[k - 1], r.sems_g, 4, k - 1, target)

    def push_rows(pg):
        rows = r.links[pl.ds(pl.multiple_of(pg * GROUP_ROWS, GROUP_ROWS), GROUP_ROWS), :]
        both = jnp.dot(rows, r.pushable[...], preferred_element_type=F32)[0:hubs_z]
        r.push[pg] = both
        r.push_p[pg] = both[:, :width].astype(BF16)
        r.push_g[pg] = both[:, width:].astype(BF16)

    loop(groups, push_rows)
    pl.semaphore_wait(barrier, zs + groups + ys - 3)
    each(zs, lambda k: gather_z(k).start())
    each(groups, lambda k: push_p(g_peer(k)[0], k).start())

    def split_count(count):
        high = count.astype(BF16).astype(F32)
        return jnp.concatenate([high, count - high], axis=0).astype(BF16)

    count = lax.dot_general(
        jnp.ones((HUB_DEV, nodes), BF16), r.links[...], WIDE, preferred_element_type=F32
    )
    for i in range(groups):
        r.push_c[i] = split_count(count[:, i * GROUP_ROWS : (i + 1) * GROUP_ROWS])
    each(groups, lambda k: push_c(g_peer(k)[0], k).start())
    each(groups, lambda k: push_g(g_peer(k)[0], k).start())

    inputs[5].wait()
    loop(nodes // GROUP_ROWS, lambda i: build(r.locals_, i * GROUP_ROWS, GROUP_ROWS, r.nbr[...]))

    inputs[4].wait()

    def self_step(i):
        rows = pl.ds(pl.multiple_of(i * CHUNK, CHUNK), CHUNK)
        r.proj_self[rows, :] = jnp.dot(r.feat[rows, :], r.w_self[...], preferred_element_type=F32)
        r.degree[rows, :] = FAN + lax.dot_general(
            r.links[:, rows], jnp.ones((s.link_cols, width), BF16), TALL, preferred_element_type=F32
        )

    loop(chunks, self_step)

    each(groups, lambda k: push_p(g_peer(k)[0], k).wait_recv())
    each(groups, lambda k: push_c(g_peer(k)[0], k).wait_recv())
    summed = r.push[g, :, 0:width]
    counts = r.push_c[g].astype(F32)
    for k in range(groups - 1):
        summed = summed + r.push_p_in[k].astype(F32)
        counts = counts + r.push_c_in[k].astype(F32)
    counts = counts[0:HUB_DEV] + counts[HUB_DEV:]
    high = counts.astype(BF16).astype(F32)
    part_row = lax.broadcasted_iota(jnp.int32, counts.shape, 0)
    parts = jnp.where(part_row == 0, high, jnp.where(part_row == 1, counts - high, 0.0))
    r.zsum_p[...] = summed.reshape(zs, HUB_DEV, width)
    for i in range(zs):
        rows = summed[i * HUB_DEV : (i + 1) * HUB_DEV]
        r.zsend_p[i] = jnp.concatenate([rows, parts], axis=0).astype(BF16)

    def push_pz(k):
        pz, target = z_peer(k)
        return copy(r.zsend_p.at[pz], r.zsend_p_in.at[k - 1], r.sems_z, 1, k - 1, target)

    each(zs, lambda k: push_pz(k).start())

    each(zs, lambda k: gather_z(k).wait_recv())
    r.hub_rows[g, 0:hubs_z] = r.own_p[...].reshape(hubs_z, width).astype(BF16)

    def gather_g(k):
        mine = r.hub_rows.at[g, pl.ds(0, hubs_z)]
        return copy(mine, mine, r.sems_g, 2, k - 1, g_peer(k)[1])

    each(groups, lambda k: gather_g(k).start())

    def near_step(i):
        rows = pl.ds(pl.multiple_of(i * CHUNK, CHUNK), CHUNK)
        r.near[rows, :] = lax.dot_general(
            r.locals_[:, rows], r.pushable[:, 0:width], TALL, preferred_element_type=F32
        )

    loop(chunks, near_step)

    each(groups, lambda k: push_g(g_peer(k)[0], k).wait_recv())
    summed = r.push[g, :, width:]
    for k in range(groups - 1):
        summed = summed + r.push_g_in[k].astype(F32)
    r.zsend_g[...] = summed.reshape(zs, HUB_DEV, width)

    def push_gz(k):
        pz, target = z_peer(k)
        return copy(r.zsend_g.at[pz], r.zsend_g_in.at[k - 1], r.sems_z, 2, k - 1, target)

    each(zs, lambda k: push_gz(k).start())

    each(groups, lambda k: gather_g(k).wait_recv())
    inputs[6].wait()

    def pull(i):
        rows = slice(i * CHUNK, (i + 1) * CHUNK)
        r.near[rows, :] = r.near[rows, :] + lax.dot_general(
            r.links[:, rows],
            r.hub_rows[...].reshape(s.link_cols, width),
            TALL,
            preferred_element_type=F32,
        )

    def activate(i):
        rows = slice(i * CHUNK, (i + 1) * CHUNK)
        picks = lax.broadcasted_iota(jnp.int32, (2 * chunks, width), 0)
        per_degree = 1.0 / r.degree[rows, :]
        pre = r.proj_self[rows, :] + r.near[rows, :] * per_degree
        sig = jax.nn.sigmoid(pre)
        act = pre * sig
        slope = sig * (1.0 + pre * (1.0 - sig))
        cot = r.cot[rows, :].astype(F32)
        r.degree[rows, :] = per_degree
        r.act[rows, :] = act
        r.act_slope[rows, :] = act * slope
        r.cot_slope[rows, :] = cot * slope
        sums = jnp.zeros((2 * chunks, CHUNK), F32)
        for at, value in ((i, act * act), (chunks + i, act * cot)):
            sums = sums + lax.dot_general(
                jnp.where(picks == at, 1.0, 0.0),
                value,
                WIDE,
                preferred_element_type=F32,
                precision=lax.Precision.HIGHEST,
            )
        return sums

    sums = jnp.zeros((2 * chunks, CHUNK), F32)
    for i in range(1, chunks):
        pull(i)
        sums = sums + activate(i)
    pull(0)

    each(zs, lambda k: push_pz(k).wait_recv())
    inflow = r.zsum_p[z]
    counts = r.zsend_p[z].astype(F32)[HUB_DEV:]
    for k in range(zs - 1):
        block = r.zsend_p_in[k].astype(F32)
        inflow = inflow + block[0:HUB_DEV]
        counts = counts + block[HUB_DEV:]
    counts = jnp.sum(counts, axis=0, keepdims=True)
    lane = lax.broadcasted_iota(jnp.int32, (HUB_DEV, GROUP_ROWS), 1)
    sub = lax.broadcasted_iota(jnp.int32, (HUB_DEV, GROUP_ROWS), 0)
    count_in = jnp.sum(jnp.where(lane == sub + z * HUB_DEV, counts, 0.0), axis=1, keepdims=True)
    r.near[0:HUB_DEV, :] = r.near[0:HUB_DEV, :] + inflow
    r.degree[0:HUB_DEV, :] = r.degree[0:HUB_DEV, :] + count_in
    r.sums[y] = sums + activate(0)

    def col_sum(buf, row):
        return lambda k: copy(buf.at[y], buf.at[y], r.sems_y, row, k - 1, y_peer(k))

    col_sums = col_sum(r.sums, 0)
    each(ys, lambda k: col_sums(k).start())

    own_f32 = r.feat[0:16, :].astype(F32)[0:HUB_DEV]
    half = s.depth // 2
    r.hub_feat[z] = jnp.concatenate([own_f32[:, :half], own_f32[:, half:]], axis=0).astype(BF16)

    def gather_f(k):
        mine = r.hub_feat.at[z]
        return copy(mine, mine, r.sems_z, 3, k - 1, z_peer(k)[1])

    each(zs, lambda k: gather_f(k).start())

    each(zs, lambda k: push_gz(k).wait_recv())
    linked = r.zsend_g[z]
    for k in range(zs - 1):
        linked = linked + r.zsend_g_in[k]
    r.own_sum[y] = linked
    spread = col_sum(r.own_sum, 1)
    each(ys, lambda k: spread(k).start())

    each(ys, lambda k: col_sums(k).wait_recv())
    sums = r.sums[0]
    for i in range(1, ys):
        sums = sums + r.sums[i]
    inv_scale = 1.0 / jnp.sqrt(sums[0:chunks] / s.depth + EPSILON)
    inner = sums[chunks:] * inv_scale / s.depth
    scales = jnp.transpose(jnp.concatenate([inv_scale, inv_scale * inv_scale * inner], axis=0))
    for i in range(chunks):
        rows = slice(i * CHUNK, (i + 1) * CHUNK)
        grad = (
            r.cot_slope[rows, :] * scales[:, i : i + 1]
            - r.act_slope[rows, :] * scales[:, chunks + i : chunks + i + 1]
        )
        r.lows[rows, 0:width] = grad.astype(BF16)
        r.scaled[rows, :] = (grad * r.degree[rows, :]).astype(BF16)

    def push2(pg, k):
        return copy(r.push2_low.at[pg], r.push2_in.at[k - 1], r.sems_g, 3, k - 1, g_peer(k)[1])

    def push2_rows(pg):
        rows = pl.ds(pl.multiple_of(pg * GROUP_ROWS, GROUP_ROWS), GROUP_ROWS)
        value = jnp.dot(r.links[rows, :], r.scaled[...], preferred_element_type=F32)
        return value[0:hubs_z]

    def push2_to(k):
        pg = g_peer(k)[0]
        r.push2_low[pg] = push2_rows(pg).astype(BF16)
        push2(pg, k).start()

    each(groups, push2_to)
    own_push2 = push2_rows(g)

    def back_step(i):
        rows = pl.ds(pl.multiple_of(i * CHUNK, CHUNK), CHUNK)
        r.lows[rows, width:] = jnp.dot(
            r.locals_[rows, :], r.scaled[...], preferred_element_type=F32
        ).astype(BF16)

    loop(chunks, back_step)

    def swap(q):
        return copy(r.part.at[1 - c, q], r.part_in.at[q], r.sems_x, 2, q, partner)

    def quarters(body):
        each(xs, lambda k: body(x_peer(k)[0]))
        body(x)

    def grad_quarter(q):
        cols = pl.ds(pl.multiple_of(q * q_rows, q_rows), q_rows)
        both = lax.dot_general(r.feat[:, cols], r.lows[...], TALL, preferred_element_type=F32)
        r.part[0, q] = both[:, :width]
        r.part[1, q] = both[:, width:]

        @pl.when(c == 1)
        def _():
            swap(q).start()

    quarters(grad_quarter)

    def send_x(k):
        px, target = x_peer(k)
        return copy(r.xsend.at[px], r.xsend_in.at[k - 1], r.sems_x, 0, k - 1, target)

    def open_x():
        def step(k):
            px = x_peer(k)[0]
            swap(px).wait_recv()
            r.xsend[px] = (r.part[c, px] + r.part_in[px]).astype(BF16)
            send_x(k).start()

        each(xs, step)
        swap(x).wait_recv()
        r.total[...] = r.part[c, x] + r.part_in[x]

    @pl.when(c == 0)
    def _():
        open_x()

    each(zs, lambda k: gather_f(k).wait_recv())
    hub_feat = r.hub_feat[...].astype(F32)
    for i in range(2):
        block = hub_feat[:, i * HUB_DEV : (i + 1) * HUB_DEV].reshape(hubs_z, half).astype(BF16)
        r.tall[0:hubs_z, i * half : (i + 1) * half] = block
        r.tall[hubs_z : 2 * hubs_z, i * half : (i + 1) * half] = block
    each(ys, lambda k: spread(k).wait_recv())
    linked = jnp.concatenate([r.own_sum[i] for i in range(ys)], axis=1)
    linked_high = linked.astype(BF16).astype(F32)
    r.tall[2 * hubs_z :, :] = jnp.concatenate([linked_high, linked - linked_high], axis=0).astype(BF16)
    own_scaled = r.scaled[0:16, :].astype(F32)[0:HUB_DEV]
    each(groups, lambda k: push2(g_peer(k)[0], k).wait_recv())
    summed = own_push2
    for k in range(groups - 1):
        summed = summed + r.push2_in[k].astype(F32)
    high = summed.astype(BF16).astype(F32)
    flat = jnp.concatenate([high, summed - high, own_scaled, own_scaled], axis=0).astype(BF16)

    def hub_quarter(q):
        cols = pl.ds(pl.multiple_of(q * q_rows, q_rows), q_rows)
        r.part[1, q] = r.part[1, q] + lax.dot_general(
            r.tall[:, cols], flat, TALL, preferred_element_type=F32
        )

        @pl.when(c == 0)
        def _():
            swap(q).start()

    quarters(hub_quarter)

    @pl.when(c == 1)
    def _():
        open_x()

    for i in range(chunks):
        rows = slice(i * CHUNK, (i + 1) * CHUNK)
        r.output[rows, :] = (r.act[rows, :] * scales[:, i : i + 1]).astype(BF16)

    put_output = pltpu.make_async_copy(r.output, out, r.sems_l.at[7])
    put_output.start()

    each(xs, lambda k: send_x(k).wait_recv())
    reduced = r.total[...]
    for k in range(xs - 1):
        reduced = reduced + r.xsend_in[k].astype(F32)
    r.quarter[...] = reduced.reshape(owners, s.o_rows, width)
    r.zq[...] = reduced.astype(BF16).reshape(owners, s.o_rows, width)

    def owns(pz):
        return lax.rem(pz, 3) != 2

    def rank(pz):
        return (pz // 3) * 2 + lax.rem(pz, 3)

    def send_q(k):
        pz, target = z_peer(k)
        return copy(r.zq.at[rank(pz)], r.zq_in.at[k - 1], r.sems_z, 4, k - 1, target)

    def wait_q(k):
        return copy(r.zq.at[0], r.zq_in.at[k - 1], r.sems_z, 4, k - 1, z_peer(k)[1])

    def send_f(k):
        mine = r.final.at[c, x, rank(z)]
        return copy(mine, mine, r.sems_z, 5, k - 1, z_peer(k)[1])

    def wait_f(k):
        piece = r.final.at[c, x, 0]
        return copy(piece, piece, r.sems_z, 5, k - 1, z_peer(k)[1])

    def send_xf(piece, k):
        mine = r.final.at[c, x, piece]
        return copy(mine, mine, r.sems_f, k - 1, piece, x_peer(k)[1])

    def start_q(k):
        @pl.when(owns(z_peer(k)[0]))
        def _():
            send_q(k).start()

    each(zs, start_q)

    each(zs, lambda k: gather_z(k).wait_send())
    each(groups, lambda k: push_p(g_peer(k)[0], k).wait_send())
    each(groups, lambda k: push_c(g_peer(k)[0], k).wait_send())
    each(groups, lambda k: push_g(g_peer(k)[0], k).wait_send())
    each(groups, lambda k: gather_g(k).wait_send())
    each(zs, lambda k: push_pz(k).wait_send())
    each(zs, lambda k: push_gz(k).wait_send())
    each(ys, lambda k: col_sums(k).wait_send())
    each(zs, lambda k: gather_f(k).wait_send())
    each(ys, lambda k: spread(k).wait_send())
    each(groups, lambda k: push2(g_peer(k)[0], k).wait_send())
    each(xs, lambda k: send_x(k).wait_send())

    @pl.when(owns(z))
    def _():
        mine = r.quarter[rank(z)]
        each_near(zs, lambda k: wait_q(k).wait_recv())
        for k in range(zs - 1):
            mine = mine + r.zq_in[k].astype(F32)
        r.final[c, x, rank(z)] = mine.astype(BF16)
        each(zs, lambda k: send_f(k).start())
        each(xs, lambda k: send_xf(rank(z), k).start())

    def arrive(k):
        source = lax.rem(z + zs - k, zs)

        @pl.when(owns(source))
        def _():
            wait_f(k).wait_recv()
            each(xs, lambda j: send_xf(rank(source), j).start())

    each_near(zs, arrive)

    def hand_over(k, px):
        piece = r.final.at[c, px]
        return copy(piece, piece, r.sems_x, 1, k, partner)

    def keep(core, px):
        return pltpu.make_async_copy(r.final.at[core, px], grads.at[core, px], r.sems_o.at[core, px])

    hand_over(0, x).start()
    keep(c, x).start()

    def pass_on(k):
        loop(owners, lambda piece: send_xf(piece, k).wait_recv())
        px = lax.rem(x + xs - k, xs)
        hand_over(k, px).start()
        keep(c, px).start()

    each_near(xs, pass_on)

    def finish_q(k):
        @pl.when(owns(z_peer(k)[0]))
        def _():
            wait_q(k).wait_send()

    each(zs, finish_q)

    @pl.when(owns(z))
    def _():
        each(zs, lambda k: wait_f(k).wait_send())

    each(xs, lambda k: loop(owners, lambda piece: send_xf(piece, k).wait_send()))
    loop(xs, lambda q: swap(q).wait_send())
    put_output.wait()

    def take(k):
        hand_over(k, 0).wait()
        keep(1 - c, lax.rem(x + xs - k, xs)).start()

    take(0)
    each_near(xs, take)
    for core in range(CORES):
        loop(xs, lambda px: keep(core, px).wait())


def finish(output_in, grads_in, output_out, self_out, neigh_out, rows, low, high, sems):
    count, half = low.shape[0], low.shape[1]
    loads = []
    stores = []
    for i in range(count):
        part = pl.ds(i % 2 * half, half)
        target = (self_out, neigh_out)[i // 2]
        loads.append(pltpu.make_async_copy(grads_in.at[i // 2, part], low.at[i], sems.at[0, i]))
        stores.append(pltpu.make_async_copy(high.at[i], target.at[part], sems.at[1, i]))
    loads.append(pltpu.make_async_copy(output_in, rows, sems.at[0, count]))
    stores.append(pltpu.make_async_copy(rows, output_out, sems.at[1, count]))
    for load in loads:
        load.start()
    for i in range(count):
        loads[i].wait()
        high[i] = low[i].astype(F32)
        stores[i].start()
    loads[count].wait()
    stores[count].start()
    for store in stores:
        store.wait()


def local(dims, features, w_self, w_neigh, local_nbr, hub_link, hub_used, cotangent):
    nodes, depth = features.shape
    s = sizes(dims, nodes, depth, w_self.shape[1])
    scratch = scratch_of(s)
    output, grads = pl.pallas_call(
        functools.partial(kernel, s, tuple(scratch)),
        out_shape=(
            jax.ShapeDtypeStruct((nodes, s.width), BF16),
            jax.ShapeDtypeStruct((CORES, s.xs, s.owners, s.o_rows, s.width), BF16),
        ),
        in_specs=[pl.BlockSpec(memory_space=pl.ANY)] * 7,
        out_specs=(pl.BlockSpec(memory_space=pl.ANY),) * 2,
        scratch_shapes=list(scratch.values()),
        compiler_params=pltpu.CompilerParams(
            collective_id=0, has_side_effects=True, vmem_limit_bytes=56 * 1024 * 1024
        ),
    )(features, w_self, w_neigh, local_nbr.T, hub_link.T, hub_used.T, cotangent)
    grad = jax.ShapeDtypeStruct((depth, s.width), F32)
    return pl.pallas_call(
        finish,
        out_shape=(jax.ShapeDtypeStruct((nodes, s.width), BF16), grad, grad),
        in_specs=[pl.BlockSpec(memory_space=pl.ANY)] * 2,
        out_specs=(pl.BlockSpec(memory_space=pl.ANY),) * 3,
        scratch_shapes=[
            pltpu.VMEM((nodes, s.width), BF16),
            pltpu.VMEM((2 * CORES, depth // 2, s.width), BF16),
            pltpu.VMEM((2 * CORES, depth // 2, s.width), F32),
            pltpu.SemaphoreType.DMA((2, 2 * CORES + 1)),
        ],
    )(output, grads.reshape(CORES, depth, s.width))


def solution(mesh):
    ys = mesh.shape["cols"]
    xs = X_CHIPS
    zs = mesh.shape["nodes"] // (xs * CORES)
    placed = (
        P("nodes", None),
        P(None, "cols"),
        P(None, "cols"),
        P("nodes", None),
        P("nodes", None),
        P("nodes", None),
        P("nodes", "cols"),
    )
    return jax.shard_map(
        functools.partial(local, (xs, zs, ys)),
        mesh=mesh,
        in_specs=placed,
        out_specs=(P("nodes", "cols"), P(None, "cols"), P(None, "cols")),
        check_vma=False,
    )
```

```python
import functools
import types

import jax
import jax.numpy as jnp
from jax import lax
from jax.experimental import pallas as pl
from jax.experimental.pallas import tpu as pltpu
from jax.sharding import PartitionSpec as P

HUB_DEV = 8
FAN = 8
CORES = 2
GROUP_ROWS = 128
CHUNK = 256
TILE = 32
EPSILON = 1e-05
X_CHIPS = 4

F32 = jnp.float32
BF16 = jnp.bfloat16
TALL = (((0,), (0,)), ((), ()))
WIDE = (((1,), (1,)), ((), ()))


def sizes(dims, nodes, depth, width):
    xs, zs, ys = dims
    s = types.SimpleNamespace(xs=xs, zs=zs, ys=ys, nodes=nodes, depth=depth, width=width)
    s.groups = xs * CORES
    s.hubs_z = zs * HUB_DEV
    s.owners = 2 * zs // 3
    s.q_rows = depth // xs
    s.o_rows = s.q_rows // s.owners
    s.link_cols = s.groups * GROUP_ROWS
    s.chunks = nodes // CHUNK
    return s


def scratch_of(s):
    vmem = pltpu.VMEM
    dma = pltpu.SemaphoreType.DMA
    w = s.width
    hub_k = 2 * s.hubs_z + 2 * HUB_DEV
    return {
        "feat": vmem((s.nodes, s.depth), BF16),
        "w_self": vmem((s.depth, w), BF16),
        "w_neigh": vmem((s.depth, w), BF16),
        "nbr": vmem((FAN, s.nodes), jnp.int32),
        "link": vmem((4, s.nodes), jnp.int32),
        "used": vmem((4, s.nodes), jnp.int32),
        "cot": vmem((s.nodes, w), BF16),
        "links": vmem((s.link_cols, s.nodes), BF16),
        "locals_": vmem((s.nodes, s.nodes), BF16),
        "proj_self": vmem((s.nodes, w), F32),
        "pushable": vmem((s.nodes, 2 * w), BF16),
        "hub_rows": vmem((s.groups, GROUP_ROWS, w), BF16),
        "near": vmem((s.nodes, w), F32),
        "degree": vmem((s.nodes, w), F32),
        "push": vmem((s.groups, s.hubs_z, 2 * w), F32),
        "push_p": vmem((s.groups, s.hubs_z, w), BF16),
        "push_p_in": vmem((s.groups - 1, s.hubs_z, w), BF16),
        "push_c": vmem((s.groups, 2 * HUB_DEV, GROUP_ROWS), BF16),
        "push_c_in": vmem((s.groups - 1, 2 * HUB_DEV, GROUP_ROWS), BF16),
        "push_g": vmem((s.groups, s.hubs_z, w), BF16),
        "push_g_in": vmem((s.groups - 1, s.hubs_z, w), BF16),
        "zsum_p": vmem((s.zs, HUB_DEV, w), F32),
        "zsend_p": vmem((s.zs, 2 * HUB_DEV, w), BF16),
        "zsend_p_in": vmem((s.zs - 1, 2 * HUB_DEV, w), BF16),
        "zsend_g": vmem((s.zs, HUB_DEV, w), F32),
        "zsend_g_in": vmem((s.zs - 1, HUB_DEV, w), F32),
        "own_p": vmem((s.zs, HUB_DEV, w), F32),
        "own_sum": vmem((s.ys, HUB_DEV, w), F32),
        "hub_feat": vmem((s.zs, 2 * HUB_DEV, s.depth // 2), BF16),
        "sums": vmem((s.ys, 2 * s.chunks, CHUNK), F32),
        "act": vmem((s.nodes, w), F32),
        "act_slope": vmem((s.nodes, w), F32),
        "cot_slope": vmem((s.nodes, w), F32),
        "lows": vmem((s.nodes, 2 * w), BF16),
        "scaled": vmem((s.nodes, w), BF16),
        "push2_low": vmem((s.groups, s.hubs_z, w), BF16),
        "push2_in": vmem((s.groups - 1, s.hubs_z, w), BF16),
        "tall": vmem((hub_k, s.depth), BF16),
        "part": vmem((CORES, s.xs, s.q_rows, w), F32),
        "part_in": vmem((s.xs, s.q_rows, w), F32),
        "total": vmem((s.q_rows, w), F32),
        "xsend": vmem((s.xs, s.q_rows, w), BF16),
        "xsend_in": vmem((s.xs - 1, s.q_rows, w), BF16),
        "quarter": vmem((s.owners, s.o_rows, w), F32),
        "zq": vmem((s.owners, s.o_rows, w), BF16),
        "zq_in": vmem((s.zs - 1, s.o_rows, w), BF16),
        "final": vmem((CORES, s.xs, s.owners, s.o_rows, w), BF16),
        "sems_z": dma((2, 6, s.zs - 1)),
        "sems_g": dma((2, 5, s.groups - 1)),
        "sems_y": dma((2, 2, s.ys - 1)),
        "sems_x": dma((2, 3, s.xs)),
        "sems_f": dma((2, s.xs - 1, s.owners)),
        "output": vmem((s.nodes, w), BF16),
        "sems_l": dma((8,)),
        "sems_o": dma((CORES, s.xs)),
    }


def kernel(s, names, feat_in, w_self_in, w_neigh_in, nbr_in, link_in, used_in, cot_in, out, grads, *refs):
    r = types.SimpleNamespace(**dict(zip(names, refs)))
    xs, zs, ys, width, nodes = s.xs, s.zs, s.ys, s.width, s.nodes
    groups, hubs_z, owners, q_rows = s.groups, s.hubs_z, s.owners, s.q_rows
    chunks = s.chunks
    me = lax.axis_index("nodes")
    y = lax.axis_index("cols")
    c = lax.rem(me, CORES)
    z = lax.rem(me // CORES, zs)
    x = me // (CORES * zs)
    g = x * CORES + c

    def node(px, pz, pc):
        return (px * zs + pz) * CORES + pc

    def copy(src, dst, sems, row, slot, target):
        return pltpu.make_async_remote_copy(
            src_ref=src,
            dst_ref=dst,
            send_sem=sems.at[0, row, slot],
            recv_sem=sems.at[1, row, slot],
            device_id=target,
            device_id_type=pl.DeviceIdType.MESH,
        )

    def loop(count, body):
        def step(i, carry):
            body(i)
            return carry

        lax.fori_loop(0, count, step, 0)

    def ranked(count, i):
        return count // 2 + (i // 2) * (1 - 2 * lax.rem(i, 2))

    def each(count, body):
        loop(count - 1, lambda i: body(ranked(count, i + 1)))

    def each_near(count, body):
        loop(count - 1, lambda i: body(ranked(count, count - 1 - i)))

    def z_peer(k):
        pz = lax.rem(z + k, zs)
        return pz, (node(x, pz, c), y)

    def g_peer(k):
        px = lax.rem(x + k // CORES, xs)
        pc = lax.rem(c + lax.rem(k, CORES), CORES)
        return px * CORES + pc, (node(px, z, pc), y)

    def y_peer(k):
        return me, lax.rem(y + k, ys)

    def x_peer(k):
        px = lax.rem(x + k, xs)
        return px, (node(px, z, c), y)

    partner = (node(x, z, 1 - c), y)

    barrier = pltpu.get_barrier_semaphore()

    def greet(target):
        pl.semaphore_signal(barrier, inc=1, device_id=target, device_id_type=pl.DeviceIdType.MESH)

    inputs = [
        pltpu.make_async_copy(src, dst, r.sems_l.at[i])
        for i, (src, dst) in enumerate(
            (
                (link_in, r.link),
                (used_in, r.used),
                (w_neigh_in, r.w_neigh),
                (feat_in, r.feat),
                (w_self_in, r.w_self),
                (nbr_in, r.nbr),
                (cot_in, r.cot),
            )
        )
    ]
    for item in inputs:
        item.start()
    each(zs, lambda k: greet(z_peer(k)[1]))
    each(ys, lambda k: greet(y_peer(k)))
    each(groups, lambda k: greet(g_peer(k)[1]))
    r.hub_rows[:, hubs_z:] = jnp.zeros((groups, GROUP_ROWS - hubs_z, width), BF16)

    def build(dest, base, count, picks):
        near_ids = (picks - base).astype(jnp.int16)
        ids = lax.broadcasted_iota(jnp.int16, (count, nodes), 0)
        acc = jnp.zeros((count, nodes), BF16)
        for k in range(picks.shape[0]):
            hit = ids == near_ids[k : k + 1, :]
            acc = acc + jnp.where(hit, jnp.bfloat16(1.0), jnp.bfloat16(0.0))
        dest[pl.ds(pl.multiple_of(base, GROUP_ROWS), count), :] = acc

    inputs[0].wait()
    inputs[1].wait()
    hub = r.link[...]
    place = lax.rem(hub, HUB_DEV)
    device = lax.div(hub, HUB_DEV)
    core = lax.rem(device, CORES)
    chip = lax.div(device, CORES)
    hub_x = jnp.zeros_like(chip)
    for i in range(1, xs):
        hub_x = hub_x + (chip >= i * zs).astype(jnp.int32)
    hub_z = chip - hub_x * zs
    column = (hub_x * CORES + core) * GROUP_ROWS + hub_z * HUB_DEV + place
    r.link[...] = jnp.where(r.used[...] > 0, column, -1)
    tiles = -(-hubs_z // TILE) * TILE

    def build_links(i):
        base = i * GROUP_ROWS
        build(r.links, base, tiles, r.link[...])
        if tiles < GROUP_ROWS:
            rest = GROUP_ROWS - tiles
            r.links[pl.ds(pl.multiple_of(base + tiles, TILE), rest), :] = jnp.zeros((rest, nodes), BF16)

    loop(groups, build_links)

    inputs[2].wait()
    inputs[3].wait()
    own_rows = r.feat[0:16, :]
    r.own_p[z] = jnp.dot(own_rows, r.w_neigh[...], preferred_element_type=F32)[0:HUB_DEV]

    def gather_z(k):
        mine = r.own_p.at[z]
        return copy(mine, mine, r.sems_z, 0, k - 1, z_peer(k)[1])

    def proj_step(i):
        rows = pl.ds(pl.multiple_of(i * CHUNK, CHUNK), CHUNK)
        r.pushable[rows, 0:width] = jnp.dot(
            r.feat[rows, :], r.w_neigh[...], preferred_element_type=F32
        ).astype(BF16)
        r.pushable[rows, width:] = r.feat[rows, pl.ds(pl.multiple_of(y * width, 128), width)]

    loop(chunks, proj_step)

    def push_p(pg, k):
        target = g_peer(k)[1]
        return copy(r.push_p.at[pg], r.push_p_in.at[k - 1], r.sems_g, 0, k - 1, target)

    def push_g(pg, k):
        target = g_peer(k)[1]
        return copy(r.push_g.at[pg], r.push_g_in.at[k - 1], r.sems_g, 1, k - 1, target)

    def push_c(pg, k):
        target = g_peer(k)[1]
        return copy(r.push_c.at[pg], r.push_c_in.at[k - 1], r.sems_g, 4, k - 1, target)

    def push_rows(pg):
        rows = r.links[pl.ds(pl.multiple_of(pg * GROUP_ROWS, GROUP_ROWS), GROUP_ROWS), :]
        both = jnp.dot(rows, r.pushable[...], preferred_element_type=F32)[0:hubs_z]
        r.push[pg] = both
        r.push_p[pg] = both[:, :width].astype(BF16)
        r.push_g[pg] = both[:, width:].astype(BF16)

    loop(groups, push_rows)
    pl.semaphore_wait(barrier, zs + groups + ys - 3)
    each(zs, lambda k: gather_z(k).start())
    each(groups, lambda k: push_p(g_peer(k)[0], k).start())

    def split_count(count):
        high = count.astype(BF16).astype(F32)
        return jnp.concatenate([high, count - high], axis=0).astype(BF16)

    count = lax.dot_general(
        jnp.ones((HUB_DEV, nodes), BF16), r.links[...], WIDE, preferred_element_type=F32
    )
    for i in range(groups):
        r.push_c[i] = split_count(count[:, i * GROUP_ROWS : (i + 1) * GROUP_ROWS])
    each(groups, lambda k: push_c(g_peer(k)[0], k).start())
    each(groups, lambda k: push_g(g_peer(k)[0], k).start())

    inputs[4].wait()

    def self_step(i):
        rows = pl.ds(pl.multiple_of(i * CHUNK, CHUNK), CHUNK)
        r.proj_self[rows, :] = jnp.dot(r.feat[rows, :], r.w_self[...], preferred_element_type=F32)
        r.degree[rows, :] = FAN + lax.dot_general(
            r.links[:, rows], jnp.ones((s.link_cols, width), BF16), TALL, preferred_element_type=F32
        )

    loop(chunks, self_step)

    each(groups, lambda k: push_p(g_peer(k)[0], k).wait_recv())
    each(groups, lambda k: push_c(g_peer(k)[0], k).wait_recv())
    summed = r.push[g, :, 0:width]
    counts = r.push_c[g].astype(F32)
    for k in range(groups - 1):
        summed = summed + r.push_p_in[k].astype(F32)
        counts = counts + r.push_c_in[k].astype(F32)
    counts = counts[0:HUB_DEV] + counts[HUB_DEV:]
    high = counts.astype(BF16).astype(F32)
    part_row = lax.broadcasted_iota(jnp.int32, counts.shape, 0)
    parts = jnp.where(part_row == 0, high, jnp.where(part_row == 1, counts - high, 0.0))
    r.zsum_p[...] = summed.reshape(zs, HUB_DEV, width)
    for i in range(zs):
        rows = summed[i * HUB_DEV : (i + 1) * HUB_DEV]
        r.zsend_p[i] = jnp.concatenate([rows, parts], axis=0).astype(BF16)

    def push_pz(k):
        pz, target = z_peer(k)
        return copy(r.zsend_p.at[pz], r.zsend_p_in.at[k - 1], r.sems_z, 1, k - 1, target)

    each(zs, lambda k: push_pz(k).start())

    each(zs, lambda k: gather_z(k).wait_recv())
    r.hub_rows[g, 0:hubs_z] = r.own_p[...].reshape(hubs_z, width).astype(BF16)

    def gather_g(k):
        mine = r.hub_rows.at[g, pl.ds(0, hubs_z)]
        return copy(mine, mine, r.sems_g, 2, k - 1, g_peer(k)[1])

    each(groups, lambda k: gather_g(k).start())

    inputs[5].wait()
    loop(nodes // GROUP_ROWS, lambda i: build(r.locals_, i * GROUP_ROWS, GROUP_ROWS, r.nbr[...]))

    def near_step(i):
        rows = pl.ds(pl.multiple_of(i * CHUNK, CHUNK), CHUNK)
        r.near[rows, :] = lax.dot_general(
            r.locals_[:, rows], r.pushable[:, 0:width], TALL, preferred_element_type=F32
        )

    loop(chunks, near_step)

    each(groups, lambda k: push_g(g_peer(k)[0], k).wait_recv())
    summed = r.push[g, :, width:]
    for k in range(groups - 1):
        summed = summed + r.push_g_in[k].astype(F32)
    r.zsend_g[...] = summed.reshape(zs, HUB_DEV, width)

    def push_gz(k):
        pz, target = z_peer(k)
        return copy(r.zsend_g.at[pz], r.zsend_g_in.at[k - 1], r.sems_z, 2, k - 1, target)

    each(zs, lambda k: push_gz(k).start())

    each(groups, lambda k: gather_g(k).wait_recv())
    inputs[6].wait()

    def pull(i):
        rows = slice(i * CHUNK, (i + 1) * CHUNK)
        r.near[rows, :] = r.near[rows, :] + lax.dot_general(
            r.links[:, rows],
            r.hub_rows[...].reshape(s.link_cols, width),
            TALL,
            preferred_element_type=F32,
        )

    def activate(i):
        rows = slice(i * CHUNK, (i + 1) * CHUNK)
        picks = lax.broadcasted_iota(jnp.int32, (CHUNK, width), 1)
        per_degree = 1.0 / r.degree[rows, :]
        pre = r.proj_self[rows, :] + r.near[rows, :] * per_degree
        sig = jax.nn.sigmoid(pre)
        act = pre * sig
        slope = sig * (1.0 + pre * (1.0 - sig))
        cot = r.cot[rows, :].astype(F32)
        r.degree[rows, :] = per_degree
        r.act[rows, :] = act
        r.act_slope[rows, :] = act * slope
        r.cot_slope[rows, :] = cot * slope
        sums = jnp.zeros((CHUNK, width), F32)
        for at, value in ((i, act * act), (chunks + i, act * cot)):
            sums = jnp.where(picks == at, jnp.sum(value, axis=1, keepdims=True), sums)
        return sums

    sums = jnp.zeros((CHUNK, width), F32)
    for i in range(1, chunks):
        pull(i)
        sums = sums + activate(i)
    pull(0)

    each(zs, lambda k: push_pz(k).wait_recv())
    inflow = r.zsum_p[z]
    counts = r.zsend_p[z].astype(F32)[HUB_DEV:]
    for k in range(zs - 1):
        block = r.zsend_p_in[k].astype(F32)
        inflow = inflow + block[0:HUB_DEV]
        counts = counts + block[HUB_DEV:]
    counts = jnp.sum(counts, axis=0, keepdims=True)
    lane = lax.broadcasted_iota(jnp.int32, (HUB_DEV, GROUP_ROWS), 1)
    sub = lax.broadcasted_iota(jnp.int32, (HUB_DEV, GROUP_ROWS), 0)
    count_in = jnp.sum(jnp.where(lane == sub + z * HUB_DEV, counts, 0.0), axis=1, keepdims=True)
    r.near[0:HUB_DEV, :] = r.near[0:HUB_DEV, :] + inflow
    r.degree[0:HUB_DEV, :] = r.degree[0:HUB_DEV, :] + count_in
    r.sums[y] = jnp.transpose(sums + activate(0))[0 : 2 * chunks]

    def col_sum(buf, row):
        return lambda k: copy(buf.at[y], buf.at[y], r.sems_y, row, k - 1, y_peer(k))

    col_sums = col_sum(r.sums, 0)
    each(ys, lambda k: col_sums(k).start())

    own_f32 = r.feat[0:16, :].astype(F32)[0:HUB_DEV]
    half = s.depth // 2
    r.hub_feat[z] = jnp.concatenate([own_f32[:, :half], own_f32[:, half:]], axis=0).astype(BF16)

    def gather_f(k):
        mine = r.hub_feat.at[z]
        return copy(mine, mine, r.sems_z, 3, k - 1, z_peer(k)[1])

    each(zs, lambda k: gather_f(k).start())

    each(zs, lambda k: push_gz(k).wait_recv())
    linked = r.zsend_g[z]
    for k in range(zs - 1):
        linked = linked + r.zsend_g_in[k]
    r.own_sum[y] = linked
    spread = col_sum(r.own_sum, 1)
    each(ys, lambda k: spread(k).start())

    each(ys, lambda k: col_sums(k).wait_recv())
    sums = r.sums[0]
    for i in range(1, ys):
        sums = sums + r.sums[i]
    inv_scale = 1.0 / jnp.sqrt(sums[0:chunks] / s.depth + EPSILON)
    inner = sums[chunks:] * inv_scale / s.depth
    scales = jnp.transpose(jnp.concatenate([inv_scale, inv_scale * inv_scale * inner], axis=0))
    for i in range(chunks):
        rows = slice(i * CHUNK, (i + 1) * CHUNK)
        grad = (
            r.cot_slope[rows, :] * scales[:, i : i + 1]
            - r.act_slope[rows, :] * scales[:, chunks + i : chunks + i + 1]
        )
        r.lows[rows, 0:width] = grad.astype(BF16)
        r.scaled[rows, :] = (grad * r.degree[rows, :]).astype(BF16)

    def push2(pg, k):
        return copy(r.push2_low.at[pg], r.push2_in.at[k - 1], r.sems_g, 3, k - 1, g_peer(k)[1])

    def push2_rows(pg):
        rows = pl.ds(pl.multiple_of(pg * GROUP_ROWS, GROUP_ROWS), GROUP_ROWS)
        value = jnp.dot(r.links[rows, :], r.scaled[...], preferred_element_type=F32)
        return value[0:hubs_z]

    def push2_to(k):
        pg = g_peer(k)[0]
        r.push2_low[pg] = push2_rows(pg).astype(BF16)
        push2(pg, k).start()

    each(groups, push2_to)
    own_push2 = push2_rows(g)

    def back_step(i):
        rows = pl.ds(pl.multiple_of(i * CHUNK, CHUNK), CHUNK)
        r.lows[rows, width:] = jnp.dot(
            r.locals_[rows, :], r.scaled[...], preferred_element_type=F32
        ).astype(BF16)

    loop(chunks, back_step)

    def swap(q):
        return copy(r.part.at[1 - c, q], r.part_in.at[q], r.sems_x, 2, q, partner)

    def quarters(body):
        each(xs, lambda k: body(x_peer(k)[0]))
        body(x)

    def grad_quarter(q):
        cols = pl.ds(pl.multiple_of(q * q_rows, q_rows), q_rows)
        both = lax.dot_general(r.feat[:, cols], r.lows[...], TALL, preferred_element_type=F32)
        r.part[0, q] = both[:, :width]
        r.part[1, q] = both[:, width:]

        @pl.when(c == 1)
        def _():
            swap(q).start()

    quarters(grad_quarter)

    def send_x(k):
        px, target = x_peer(k)
        return copy(r.xsend.at[px], r.xsend_in.at[k - 1], r.sems_x, 0, k - 1, target)

    def open_x():
        def step(k):
            px = x_peer(k)[0]
            swap(px).wait_recv()
            r.xsend[px] = (r.part[c, px] + r.part_in[px]).astype(BF16)
            send_x(k).start()

        each(xs, step)
        swap(x).wait_recv()
        r.total[...] = r.part[c, x] + r.part_in[x]

    @pl.when(c == 0)
    def _():
        open_x()

    each(zs, lambda k: gather_f(k).wait_recv())
    hub_feat = r.hub_feat[...].astype(F32)
    for i in range(2):
        block = hub_feat[:, i * HUB_DEV : (i + 1) * HUB_DEV].reshape(hubs_z, half).astype(BF16)
        r.tall[0:hubs_z, i * half : (i + 1) * half] = block
        r.tall[hubs_z : 2 * hubs_z, i * half : (i + 1) * half] = block
    each(ys, lambda k: spread(k).wait_recv())
    linked = jnp.concatenate([r.own_sum[i] for i in range(ys)], axis=1)
    linked_high = linked.astype(BF16).astype(F32)
    r.tall[2 * hubs_z :, :] = jnp.concatenate([linked_high, linked - linked_high], axis=0).astype(BF16)
    own_scaled = r.scaled[0:16, :].astype(F32)[0:HUB_DEV]
    each(groups, lambda k: push2(g_peer(k)[0], k).wait_recv())
    summed = own_push2
    for k in range(groups - 1):
        summed = summed + r.push2_in[k].astype(F32)
    high = summed.astype(BF16).astype(F32)
    flat = jnp.concatenate([high, summed - high, own_scaled, own_scaled], axis=0).astype(BF16)

    def hub_quarter(q):
        cols = pl.ds(pl.multiple_of(q * q_rows, q_rows), q_rows)
        r.part[1, q] = r.part[1, q] + lax.dot_general(
            r.tall[:, cols], flat, TALL, preferred_element_type=F32
        )

        @pl.when(c == 0)
        def _():
            swap(q).start()

    quarters(hub_quarter)

    @pl.when(c == 1)
    def _():
        open_x()

    for i in range(chunks):
        rows = slice(i * CHUNK, (i + 1) * CHUNK)
        r.output[rows, :] = (r.act[rows, :] * scales[:, i : i + 1]).astype(BF16)

    put_output = pltpu.make_async_copy(r.output, out, r.sems_l.at[7])
    put_output.start()

    each(xs, lambda k: send_x(k).wait_recv())
    reduced = r.total[...]
    for k in range(xs - 1):
        reduced = reduced + r.xsend_in[k].astype(F32)
    r.quarter[...] = reduced.reshape(owners, s.o_rows, width)
    r.zq[...] = reduced.astype(BF16).reshape(owners, s.o_rows, width)

    def owns(pz):
        return lax.rem(pz, 3) != 2

    def rank(pz):
        return (pz // 3) * 2 + lax.rem(pz, 3)

    def send_q(k):
        pz, target = z_peer(k)
        return copy(r.zq.at[rank(pz)], r.zq_in.at[k - 1], r.sems_z, 4, k - 1, target)

    def wait_q(k):
        return copy(r.zq.at[0], r.zq_in.at[k - 1], r.sems_z, 4, k - 1, z_peer(k)[1])

    def send_f(k):
        mine = r.final.at[c, x, rank(z)]
        return copy(mine, mine, r.sems_z, 5, k - 1, z_peer(k)[1])

    def wait_f(k):
        piece = r.final.at[c, x, 0]
        return copy(piece, piece, r.sems_z, 5, k - 1, z_peer(k)[1])

    def send_xf(piece, k):
        mine = r.final.at[c, x, piece]
        return copy(mine, mine, r.sems_f, k - 1, piece, x_peer(k)[1])

    def start_q(k):
        @pl.when(owns(z_peer(k)[0]))
        def _():
            send_q(k).start()

    each(zs, start_q)

    each(zs, lambda k: gather_z(k).wait_send())
    each(groups, lambda k: push_p(g_peer(k)[0], k).wait_send())
    each(groups, lambda k: push_c(g_peer(k)[0], k).wait_send())
    each(groups, lambda k: push_g(g_peer(k)[0], k).wait_send())
    each(groups, lambda k: gather_g(k).wait_send())
    each(zs, lambda k: push_pz(k).wait_send())
    each(zs, lambda k: push_gz(k).wait_send())
    each(ys, lambda k: col_sums(k).wait_send())
    each(zs, lambda k: gather_f(k).wait_send())
    each(ys, lambda k: spread(k).wait_send())
    each(groups, lambda k: push2(g_peer(k)[0], k).wait_send())
    each(xs, lambda k: send_x(k).wait_send())

    @pl.when(owns(z))
    def _():
        mine = r.quarter[rank(z)]
        each_near(zs, lambda k: wait_q(k).wait_recv())
        for k in range(zs - 1):
            mine = mine + r.zq_in[k].astype(F32)
        r.final[c, x, rank(z)] = mine.astype(BF16)
        each(zs, lambda k: send_f(k).start())
        each(xs, lambda k: send_xf(rank(z), k).start())

    def arrive(k):
        source = lax.rem(z + zs - k, zs)

        @pl.when(owns(source))
        def _():
            wait_f(k).wait_recv()
            each(xs, lambda j: send_xf(rank(source), j).start())

    each_near(zs, arrive)

    def hand_over(k, px):
        piece = r.final.at[c, px]
        return copy(piece, grads.at[c, px], r.sems_x, 1, k, partner)

    def keep(core, px):
        return pltpu.make_async_copy(r.final.at[core, px], grads.at[core, px], r.sems_o.at[core, px])

    hand_over(0, x).start()
    keep(c, x).start()

    def pass_on(k):
        loop(owners, lambda piece: send_xf(piece, k).wait_recv())
        px = lax.rem(x + xs - k, xs)
        hand_over(k, px).start()
        keep(c, px).start()

    each_near(xs, pass_on)

    def finish_q(k):
        @pl.when(owns(z_peer(k)[0]))
        def _():
            wait_q(k).wait_send()

    each(zs, finish_q)

    @pl.when(owns(z))
    def _():
        each(zs, lambda k: wait_f(k).wait_send())

    each(xs, lambda k: loop(owners, lambda piece: send_xf(piece, k).wait_send()))
    loop(xs, lambda q: swap(q).wait_send())
    put_output.wait()

    loop(xs, lambda k: hand_over(k, 0).wait())
    loop(xs, lambda px: keep(c, px).wait())


def finish(output_in, grads_in, output_out, self_out, neigh_out, rows, low, high, sems):
    count, half = low.shape[0], low.shape[1]
    loads = []
    stores = []
    for i in range(count):
        part = pl.ds(i % 2 * half, half)
        target = (self_out, neigh_out)[i // 2]
        loads.append(pltpu.make_async_copy(grads_in.at[i // 2, part], low.at[i], sems.at[0, i]))
        stores.append(pltpu.make_async_copy(high.at[i], target.at[part], sems.at[1, i]))
    loads.append(pltpu.make_async_copy(output_in, rows, sems.at[0, count]))
    stores.append(pltpu.make_async_copy(rows, output_out, sems.at[1, count]))
    for load in loads:
        load.start()
    for i in range(count):
        loads[i].wait()
        high[i] = low[i].astype(F32)
        stores[i].start()
    loads[count].wait()
    stores[count].start()
    for store in stores:
        store.wait()


def local(dims, features, w_self, w_neigh, local_nbr, hub_link, hub_used, cotangent):
    nodes, depth = features.shape
    s = sizes(dims, nodes, depth, w_self.shape[1])
    scratch = scratch_of(s)
    output, grads = pl.pallas_call(
        functools.partial(kernel, s, tuple(scratch)),
        out_shape=(
            jax.ShapeDtypeStruct((nodes, s.width), BF16),
            jax.ShapeDtypeStruct((CORES, s.xs, s.owners, s.o_rows, s.width), BF16),
        ),
        in_specs=[pl.BlockSpec(memory_space=pl.ANY)] * 7,
        out_specs=(pl.BlockSpec(memory_space=pl.ANY),) * 2,
        scratch_shapes=list(scratch.values()),
        compiler_params=pltpu.CompilerParams(
            collective_id=0, has_side_effects=True, vmem_limit_bytes=56 * 1024 * 1024
        ),
    )(features, w_self, w_neigh, local_nbr.T, hub_link.T, hub_used.T, cotangent)
    grad = jax.ShapeDtypeStruct((depth, s.width), F32)
    return pl.pallas_call(
        finish,
        out_shape=(jax.ShapeDtypeStruct((nodes, s.width), BF16), grad, grad),
        in_specs=[pl.BlockSpec(memory_space=pl.ANY)] * 2,
        out_specs=(pl.BlockSpec(memory_space=pl.ANY),) * 3,
        scratch_shapes=[
            pltpu.VMEM((nodes, s.width), BF16),
            pltpu.VMEM((2 * CORES, depth // 2, s.width), BF16),
            pltpu.VMEM((2 * CORES, depth // 2, s.width), F32),
            pltpu.SemaphoreType.DMA((2, 2 * CORES + 1)),
        ],
    )(output, grads.reshape(CORES, depth, s.width))


def solution(mesh):
    ys = mesh.shape["cols"]
    xs = X_CHIPS
    zs = mesh.shape["nodes"] // (xs * CORES)
    placed = (
        P("nodes", None),
        P(None, "cols"),
        P(None, "cols"),
        P("nodes", None),
        P("nodes", None),
        P("nodes", None),
        P("nodes", "cols"),
    )
    return jax.shard_map(
        functools.partial(local, (xs, zs, ys)),
        mesh=mesh,
        in_specs=placed,
        out_specs=(P("nodes", "cols"), P(None, "cols"), P(None, "cols")),
        check_vma=False,
    )
```

```python
import functools
import types

import jax
import jax.numpy as jnp
from jax import lax
from jax.experimental import pallas as pl
from jax.experimental.pallas import tpu as pltpu
from jax.sharding import PartitionSpec as P

HUB_DEV = 8
FAN = 8
CORES = 2
GROUP_ROWS = 128
CHUNK = 256
TILE = 32
EPSILON = 1e-05
X_CHIPS = 4

F32 = jnp.float32
BF16 = jnp.bfloat16
TALL = (((0,), (0,)), ((), ()))
WIDE = (((1,), (1,)), ((), ()))


def sizes(dims, nodes, depth, width):
    xs, zs, ys = dims
    s = types.SimpleNamespace(xs=xs, zs=zs, ys=ys, nodes=nodes, depth=depth, width=width)
    s.groups = xs * CORES
    s.hubs_z = zs * HUB_DEV
    s.owners = 2 * zs // 3
    s.q_rows = depth // xs
    s.o_rows = s.q_rows // s.owners
    s.link_cols = s.groups * GROUP_ROWS
    s.chunks = nodes // CHUNK
    return s


def scratch_of(s):
    vmem = pltpu.VMEM
    dma = pltpu.SemaphoreType.DMA
    w = s.width
    hub_k = 2 * s.hubs_z + 2 * HUB_DEV
    return {
        "feat": vmem((s.nodes, s.depth), BF16),
        "w_self": vmem((s.depth, w), BF16),
        "w_neigh": vmem((s.depth, w), BF16),
        "nbr": vmem((FAN, s.nodes), jnp.int32),
        "link": vmem((4, s.nodes), jnp.int32),
        "used": vmem((4, s.nodes), jnp.int32),
        "cot": vmem((s.nodes, w), BF16),
        "links": vmem((s.link_cols, s.nodes), BF16),
        "locals_": vmem((s.nodes, s.nodes), BF16),
        "proj_self": vmem((s.nodes, w), F32),
        "pushable": vmem((s.nodes, 2 * w), BF16),
        "hub_rows": vmem((s.groups, GROUP_ROWS, w), BF16),
        "near": vmem((s.nodes, w), F32),
        "degree": vmem((s.nodes, w), F32),
        "push": vmem((s.groups, s.hubs_z, 2 * w), F32),
        "push_p": vmem((s.groups, s.hubs_z, w), BF16),
        "push_p_in": vmem((s.groups - 1, s.hubs_z, w), BF16),
        "push_c": vmem((s.groups, 2 * HUB_DEV, GROUP_ROWS), BF16),
        "push_c_in": vmem((s.groups - 1, 2 * HUB_DEV, GROUP_ROWS), BF16),
        "push_g": vmem((s.groups, s.hubs_z, w), BF16),
        "push_g_in": vmem((s.groups - 1, s.hubs_z, w), BF16),
        "zsum_p": vmem((s.zs, HUB_DEV, w), F32),
        "zsend_p": vmem((s.zs, 2 * HUB_DEV, w), BF16),
        "zsend_p_in": vmem((s.zs - 1, 2 * HUB_DEV, w), BF16),
        "zsend_g": vmem((s.zs, HUB_DEV, w), F32),
        "zsend_g_in": vmem((s.zs - 1, HUB_DEV, w), F32),
        "own_p": vmem((s.zs, HUB_DEV, w), F32),
        "own_sum": vmem((s.ys, HUB_DEV, w), F32),
        "hub_feat": vmem((s.zs, 2 * HUB_DEV, s.depth // 2), BF16),
        "sums": vmem((s.ys, 2 * s.chunks, CHUNK), F32),
        "act": vmem((s.nodes, w), F32),
        "act_slope": vmem((s.nodes, w), F32),
        "cot_slope": vmem((s.nodes, w), F32),
        "lows": vmem((s.nodes, 2 * w), BF16),
        "scaled": vmem((s.nodes, w), BF16),
        "push2_low": vmem((s.groups, s.hubs_z, w), BF16),
        "push2_in": vmem((s.groups - 1, s.hubs_z, w), BF16),
        "tall": vmem((hub_k, s.depth), BF16),
        "part": vmem((CORES, s.xs, s.q_rows, w), F32),
        "part_in": vmem((s.xs, s.q_rows, w), F32),
        "total": vmem((s.q_rows, w), F32),
        "xsend": vmem((s.xs, s.q_rows, w), BF16),
        "xsend_in": vmem((s.xs - 1, s.q_rows, w), BF16),
        "quarter": vmem((s.owners, s.o_rows, w), F32),
        "zq": vmem((s.owners, s.o_rows, w), BF16),
        "zq_in": vmem((s.zs - 1, s.o_rows, w), BF16),
        "final": vmem((CORES, s.xs, s.owners, s.o_rows, w), BF16),
        "sems_z": dma((2, 6, s.zs - 1)),
        "sems_g": dma((2, 5, s.groups - 1)),
        "sems_y": dma((2, 2, s.ys - 1)),
        "sems_x": dma((2, 3, s.xs)),
        "sems_f": dma((2, s.xs - 1, s.owners)),
        "output": vmem((s.nodes, w), BF16),
        "sems_l": dma((8,)),
        "sems_o": dma((CORES, s.xs)),
    }


def kernel(s, names, feat_in, w_self_in, w_neigh_in, nbr_in, link_in, used_in, cot_in, out, grads, *refs):
    r = types.SimpleNamespace(**dict(zip(names, refs)))
    xs, zs, ys, width, nodes = s.xs, s.zs, s.ys, s.width, s.nodes
    groups, hubs_z, owners, q_rows = s.groups, s.hubs_z, s.owners, s.q_rows
    chunks = s.chunks
    me = lax.axis_index("nodes")
    y = lax.axis_index("cols")
    c = lax.rem(me, CORES)
    z = lax.rem(me // CORES, zs)
    x = me // (CORES * zs)
    g = x * CORES + c

    def node(px, pz, pc):
        return (px * zs + pz) * CORES + pc

    def copy(src, dst, sems, row, slot, target):
        return pltpu.make_async_remote_copy(
            src_ref=src,
            dst_ref=dst,
            send_sem=sems.at[0, row, slot],
            recv_sem=sems.at[1, row, slot],
            device_id=target,
            device_id_type=pl.DeviceIdType.MESH,
        )

    def loop(count, body):
        def step(i, carry):
            body(i)
            return carry

        lax.fori_loop(0, count, step, 0)

    def ranked(count, i):
        return count // 2 + (i // 2) * (1 - 2 * lax.rem(i, 2))

    def each(count, body):
        loop(count - 1, lambda i: body(ranked(count, i + 1)))

    def each_near(count, body):
        loop(count - 1, lambda i: body(ranked(count, count - 1 - i)))

    def z_peer(k):
        pz = lax.rem(z + k, zs)
        return pz, (node(x, pz, c), y)

    def g_peer(k):
        px = lax.rem(x + k // CORES, xs)
        pc = lax.rem(c + lax.rem(k, CORES), CORES)
        return px * CORES + pc, (node(px, z, pc), y)

    def y_peer(k):
        return me, lax.rem(y + k, ys)

    def x_peer(k):
        px = lax.rem(x + k, xs)
        return px, (node(px, z, c), y)

    partner = (node(x, z, 1 - c), y)

    barrier = pltpu.get_barrier_semaphore()

    def greet(target):
        pl.semaphore_signal(barrier, inc=1, device_id=target, device_id_type=pl.DeviceIdType.MESH)

    inputs = [
        pltpu.make_async_copy(src, dst, r.sems_l.at[i])
        for i, (src, dst) in enumerate(
            (
                (link_in, r.link),
                (used_in, r.used),
                (w_neigh_in, r.w_neigh),
                (feat_in, r.feat),
                (w_self_in, r.w_self),
                (nbr_in, r.nbr),
                (cot_in, r.cot),
            )
        )
    ]
    for item in inputs:
        item.start()
    each(zs, lambda k: greet(z_peer(k)[1]))
    each(ys, lambda k: greet(y_peer(k)))
    each(groups, lambda k: greet(g_peer(k)[1]))
    r.hub_rows[:, hubs_z:] = jnp.zeros((groups, GROUP_ROWS - hubs_z, width), BF16)

    def build(dest, base, count, picks):
        near_ids = (picks - base).astype(jnp.int16)
        ids = lax.broadcasted_iota(jnp.int16, (count, nodes), 0)
        acc = jnp.zeros((count, nodes), BF16)
        for k in range(picks.shape[0]):
            hit = ids == near_ids[k : k + 1, :]
            acc = acc + jnp.where(hit, jnp.bfloat16(1.0), jnp.bfloat16(0.0))
        dest[pl.ds(pl.multiple_of(base, GROUP_ROWS), count), :] = acc

    inputs[0].wait()
    inputs[1].wait()
    hub = r.link[...]
    place = lax.rem(hub, HUB_DEV)
    device = lax.div(hub, HUB_DEV)
    core = lax.rem(device, CORES)
    chip = lax.div(device, CORES)
    hub_x = jnp.zeros_like(chip)
    for i in range(1, xs):
        hub_x = hub_x + (chip >= i * zs).astype(jnp.int32)
    hub_z = chip - hub_x * zs
    column = (hub_x * CORES + core) * GROUP_ROWS + hub_z * HUB_DEV + place
    r.link[...] = jnp.where(r.used[...] > 0, column, -1)
    tiles = -(-hubs_z // TILE) * TILE

    def build_links(i):
        base = i * GROUP_ROWS
        build(r.links, base, tiles, r.link[...])
        if tiles < GROUP_ROWS:
            rest = GROUP_ROWS - tiles
            r.links[pl.ds(pl.multiple_of(base + tiles, TILE), rest), :] = jnp.zeros((rest, nodes), BF16)

    loop(groups, build_links)

    inputs[2].wait()
    inputs[3].wait()
    own_rows = r.feat[0:16, :]
    r.own_p[z] = jnp.dot(own_rows, r.w_neigh[...], preferred_element_type=F32)[0:HUB_DEV]

    def gather_z(k):
        mine = r.own_p.at[z]
        return copy(mine, mine, r.sems_z, 0, k - 1, z_peer(k)[1])

    def proj_step(i):
        rows = pl.ds(pl.multiple_of(i * CHUNK, CHUNK), CHUNK)
        r.pushable[rows, 0:width] = jnp.dot(
            r.feat[rows, :], r.w_neigh[...], preferred_element_type=F32
        ).astype(BF16)
        r.pushable[rows, width:] = r.feat[rows, pl.ds(pl.multiple_of(y * width, 128), width)]

    loop(chunks, proj_step)

    def push_p(pg, k):
        target = g_peer(k)[1]
        return copy(r.push_p.at[pg], r.push_p_in.at[k - 1], r.sems_g, 0, k - 1, target)

    def push_g(pg, k):
        target = g_peer(k)[1]
        return copy(r.push_g.at[pg], r.push_g_in.at[k - 1], r.sems_g, 1, k - 1, target)

    def push_c(pg, k):
        target = g_peer(k)[1]
        return copy(r.push_c.at[pg], r.push_c_in.at[k - 1], r.sems_g, 4, k - 1, target)

    def push_rows(pg):
        rows = r.links[pl.ds(pl.multiple_of(pg * GROUP_ROWS, GROUP_ROWS), GROUP_ROWS), :]
        both = jnp.dot(rows, r.pushable[...], preferred_element_type=F32)[0:hubs_z]
        r.push[pg] = both
        r.push_p[pg] = both[:, :width].astype(BF16)
        r.push_g[pg] = both[:, width:].astype(BF16)

    loop(groups, push_rows)
    pl.semaphore_wait(barrier, zs + groups + ys - 3)
    each(groups, lambda k: push_p(g_peer(k)[0], k).start())
    each(zs, lambda k: gather_z(k).start())

    def split_count(count):
        high = count.astype(BF16).astype(F32)
        return jnp.concatenate([high, count - high], axis=0).astype(BF16)

    count = lax.dot_general(
        jnp.ones((HUB_DEV, nodes), BF16), r.links[...], WIDE, preferred_element_type=F32
    )
    for i in range(groups):
        r.push_c[i] = split_count(count[:, i * GROUP_ROWS : (i + 1) * GROUP_ROWS])
    each(groups, lambda k: push_c(g_peer(k)[0], k).start())
    each(groups, lambda k: push_g(g_peer(k)[0], k).start())

    inputs[4].wait()

    def self_step(i):
        rows = pl.ds(pl.multiple_of(i * CHUNK, CHUNK), CHUNK)
        r.proj_self[rows, :] = jnp.dot(r.feat[rows, :], r.w_self[...], preferred_element_type=F32)
        r.degree[rows, :] = FAN + lax.dot_general(
            r.links[:, rows], jnp.ones((s.link_cols, width), BF16), TALL, preferred_element_type=F32
        )

    loop(chunks, self_step)

    each(groups, lambda k: push_p(g_peer(k)[0], k).wait_recv())
    each(groups, lambda k: push_c(g_peer(k)[0], k).wait_recv())
    summed = r.push[g, :, 0:width]
    counts = r.push_c[g].astype(F32)
    for k in range(groups - 1):
        summed = summed + r.push_p_in[k].astype(F32)
        counts = counts + r.push_c_in[k].astype(F32)
    counts = counts[0:HUB_DEV] + counts[HUB_DEV:]
    high = counts.astype(BF16).astype(F32)
    part_row = lax.broadcasted_iota(jnp.int32, counts.shape, 0)
    parts = jnp.where(part_row == 0, high, jnp.where(part_row == 1, counts - high, 0.0))
    r.zsum_p[...] = summed.reshape(zs, HUB_DEV, width)
    for i in range(zs):
        rows = summed[i * HUB_DEV : (i + 1) * HUB_DEV]
        r.zsend_p[i] = jnp.concatenate([rows, parts], axis=0).astype(BF16)

    def push_pz(k):
        pz, target = z_peer(k)
        return copy(r.zsend_p.at[pz], r.zsend_p_in.at[k - 1], r.sems_z, 1, k - 1, target)

    each(zs, lambda k: push_pz(k).start())

    each(zs, lambda k: gather_z(k).wait_recv())
    r.hub_rows[g, 0:hubs_z] = r.own_p[...].reshape(hubs_z, width).astype(BF16)

    def gather_g(k):
        mine = r.hub_rows.at[g, pl.ds(0, hubs_z)]
        return copy(mine, mine, r.sems_g, 2, k - 1, g_peer(k)[1])

    each(groups, lambda k: gather_g(k).start())

    inputs[5].wait()
    loop(nodes // GROUP_ROWS, lambda i: build(r.locals_, i * GROUP_ROWS, GROUP_ROWS, r.nbr[...]))

    def near_step(i):
        rows = pl.ds(pl.multiple_of(i * CHUNK, CHUNK), CHUNK)
        r.near[rows, :] = lax.dot_general(
            r.locals_[:, rows], r.pushable[:, 0:width], TALL, preferred_element_type=F32
        )

    loop(chunks, near_step)

    each(groups, lambda k: push_g(g_peer(k)[0], k).wait_recv())
    summed = r.push[g, :, width:]
    for k in range(groups - 1):
        summed = summed + r.push_g_in[k].astype(F32)
    r.zsend_g[...] = summed.reshape(zs, HUB_DEV, width)

    def push_gz(k):
        pz, target = z_peer(k)
        return copy(r.zsend_g.at[pz], r.zsend_g_in.at[k - 1], r.sems_z, 2, k - 1, target)

    each(zs, lambda k: push_gz(k).start())

    each(groups, lambda k: gather_g(k).wait_recv())
    inputs[6].wait()

    def pull(i):
        rows = slice(i * CHUNK, (i + 1) * CHUNK)
        r.near[rows, :] = r.near[rows, :] + lax.dot_general(
            r.links[:, rows],
            r.hub_rows[...].reshape(s.link_cols, width),
            TALL,
            preferred_element_type=F32,
        )

    def activate(i):
        rows = slice(i * CHUNK, (i + 1) * CHUNK)
        picks = lax.broadcasted_iota(jnp.int32, (CHUNK, width), 1)
        per_degree = 1.0 / r.degree[rows, :]
        pre = r.proj_self[rows, :] + r.near[rows, :] * per_degree
        sig = jax.nn.sigmoid(pre)
        act = pre * sig
        slope = sig * (1.0 + pre * (1.0 - sig))
        cot = r.cot[rows, :].astype(F32)
        r.degree[rows, :] = per_degree
        r.act[rows, :] = act
        r.act_slope[rows, :] = act * slope
        r.cot_slope[rows, :] = cot * slope
        sums = jnp.zeros((CHUNK, width), F32)
        for at, value in ((i, act * act), (chunks + i, act * cot)):
            sums = jnp.where(picks == at, jnp.sum(value, axis=1, keepdims=True), sums)
        return sums

    sums = jnp.zeros((CHUNK, width), F32)
    for i in range(1, chunks):
        pull(i)
        sums = sums + activate(i)
    pull(0)

    each(zs, lambda k: push_pz(k).wait_recv())
    inflow = r.zsum_p[z]
    counts = r.zsend_p[z].astype(F32)[HUB_DEV:]
    for k in range(zs - 1):
        block = r.zsend_p_in[k].astype(F32)
        inflow = inflow + block[0:HUB_DEV]
        counts = counts + block[HUB_DEV:]
    counts = jnp.sum(counts, axis=0, keepdims=True)
    lane = lax.broadcasted_iota(jnp.int32, (HUB_DEV, GROUP_ROWS), 1)
    sub = lax.broadcasted_iota(jnp.int32, (HUB_DEV, GROUP_ROWS), 0)
    count_in = jnp.sum(jnp.where(lane == sub + z * HUB_DEV, counts, 0.0), axis=1, keepdims=True)
    r.near[0:HUB_DEV, :] = r.near[0:HUB_DEV, :] + inflow
    r.degree[0:HUB_DEV, :] = r.degree[0:HUB_DEV, :] + count_in
    r.sums[y] = jnp.transpose(sums + activate(0))[0 : 2 * chunks]

    def col_sum(buf, row):
        return lambda k: copy(buf.at[y], buf.at[y], r.sems_y, row, k - 1, y_peer(k))

    col_sums = col_sum(r.sums, 0)
    each(ys, lambda k: col_sums(k).start())

    own_f32 = r.feat[0:16, :].astype(F32)[0:HUB_DEV]
    half = s.depth // 2
    r.hub_feat[z] = jnp.concatenate([own_f32[:, :half], own_f32[:, half:]], axis=0).astype(BF16)

    def gather_f(k):
        mine = r.hub_feat.at[z]
        return copy(mine, mine, r.sems_z, 3, k - 1, z_peer(k)[1])

    each(zs, lambda k: gather_f(k).start())

    each(zs, lambda k: push_gz(k).wait_recv())
    linked = r.zsend_g[z]
    for k in range(zs - 1):
        linked = linked + r.zsend_g_in[k]
    r.own_sum[y] = linked
    spread = col_sum(r.own_sum, 1)
    each(ys, lambda k: spread(k).start())

    each(ys, lambda k: col_sums(k).wait_recv())
    sums = r.sums[0]
    for i in range(1, ys):
        sums = sums + r.sums[i]
    inv_scale = 1.0 / jnp.sqrt(sums[0:chunks] / s.depth + EPSILON)
    inner = sums[chunks:] * inv_scale / s.depth
    scales = jnp.transpose(jnp.concatenate([inv_scale, inv_scale * inv_scale * inner], axis=0))
    for i in range(chunks):
        rows = slice(i * CHUNK, (i + 1) * CHUNK)
        grad = (
            r.cot_slope[rows, :] * scales[:, i : i + 1]
            - r.act_slope[rows, :] * scales[:, chunks + i : chunks + i + 1]
        )
        r.lows[rows, 0:width] = grad.astype(BF16)
        r.scaled[rows, :] = (grad * r.degree[rows, :]).astype(BF16)

    def push2(pg, k):
        return copy(r.push2_low.at[pg], r.push2_in.at[k - 1], r.sems_g, 3, k - 1, g_peer(k)[1])

    def push2_rows(pg):
        rows = pl.ds(pl.multiple_of(pg * GROUP_ROWS, GROUP_ROWS), GROUP_ROWS)
        value = jnp.dot(r.links[rows, :], r.scaled[...], preferred_element_type=F32)
        return value[0:hubs_z]

    def push2_to(k):
        pg = g_peer(k)[0]
        r.push2_low[pg] = push2_rows(pg).astype(BF16)
        push2(pg, k).start()

    each(groups, push2_to)
    own_push2 = push2_rows(g)

    def back_step(i):
        rows = pl.ds(pl.multiple_of(i * CHUNK, CHUNK), CHUNK)
        r.lows[rows, width:] = jnp.dot(
            r.locals_[rows, :], r.scaled[...], preferred_element_type=F32
        ).astype(BF16)

    loop(chunks, back_step)

    def swap(q):
        return copy(r.part.at[1 - c, q], r.part_in.at[q], r.sems_x, 2, q, partner)

    def quarters(body):
        each(xs, lambda k: body(x_peer(k)[0]))
        body(x)

    def grad_quarter(q):
        cols = pl.ds(pl.multiple_of(q * q_rows, q_rows), q_rows)
        both = lax.dot_general(r.feat[:, cols], r.lows[...], TALL, preferred_element_type=F32)
        r.part[0, q] = both[:, :width]
        r.part[1, q] = both[:, width:]

        @pl.when(c == 1)
        def _():
            swap(q).start()

    quarters(grad_quarter)

    def send_x(k):
        px, target = x_peer(k)
        return copy(r.xsend.at[px], r.xsend_in.at[k - 1], r.sems_x, 0, k - 1, target)

    def open_x():
        def step(k):
            px = x_peer(k)[0]
            swap(px).wait_recv()
            r.xsend[px] = (r.part[c, px] + r.part_in[px]).astype(BF16)
            send_x(k).start()

        each(xs, step)
        swap(x).wait_recv()
        r.total[...] = r.part[c, x] + r.part_in[x]

    @pl.when(c == 0)
    def _():
        open_x()

    each(zs, lambda k: gather_f(k).wait_recv())
    hub_feat = r.hub_feat[...].astype(F32)
    for i in range(2):
        block = hub_feat[:, i * HUB_DEV : (i + 1) * HUB_DEV].reshape(hubs_z, half).astype(BF16)
        r.tall[0:hubs_z, i * half : (i + 1) * half] = block
        r.tall[hubs_z : 2 * hubs_z, i * half : (i + 1) * half] = block
    each(ys, lambda k: spread(k).wait_recv())
    linked = jnp.concatenate([r.own_sum[i] for i in range(ys)], axis=1)
    linked_high = linked.astype(BF16).astype(F32)
    r.tall[2 * hubs_z :, :] = jnp.concatenate([linked_high, linked - linked_high], axis=0).astype(BF16)
    own_scaled = r.scaled[0:16, :].astype(F32)[0:HUB_DEV]
    each(groups, lambda k: push2(g_peer(k)[0], k).wait_recv())
    summed = own_push2
    for k in range(groups - 1):
        summed = summed + r.push2_in[k].astype(F32)
    high = summed.astype(BF16).astype(F32)
    flat = jnp.concatenate([high, summed - high, own_scaled, own_scaled], axis=0).astype(BF16)

    def hub_quarter(q):
        cols = pl.ds(pl.multiple_of(q * q_rows, q_rows), q_rows)
        r.part[1, q] = r.part[1, q] + lax.dot_general(
            r.tall[:, cols], flat, TALL, preferred_element_type=F32
        )

        @pl.when(c == 0)
        def _():
            swap(q).start()

    quarters(hub_quarter)

    @pl.when(c == 1)
    def _():
        open_x()

    for i in range(chunks):
        rows = slice(i * CHUNK, (i + 1) * CHUNK)
        r.output[rows, :] = (r.act[rows, :] * scales[:, i : i + 1]).astype(BF16)

    put_output = pltpu.make_async_copy(r.output, out, r.sems_l.at[7])
    put_output.start()

    each(xs, lambda k: send_x(k).wait_recv())
    reduced = r.total[...]
    for k in range(xs - 1):
        reduced = reduced + r.xsend_in[k].astype(F32)
    r.quarter[...] = reduced.reshape(owners, s.o_rows, width)
    r.zq[...] = reduced.astype(BF16).reshape(owners, s.o_rows, width)

    def owns(pz):
        return lax.rem(pz, 3) != 2

    def rank(pz):
        return (pz // 3) * 2 + lax.rem(pz, 3)

    def send_q(k):
        pz, target = z_peer(k)
        return copy(r.zq.at[rank(pz)], r.zq_in.at[k - 1], r.sems_z, 4, k - 1, target)

    def wait_q(k):
        return copy(r.zq.at[0], r.zq_in.at[k - 1], r.sems_z, 4, k - 1, z_peer(k)[1])

    def send_f(k):
        mine = r.final.at[c, x, rank(z)]
        return copy(mine, mine, r.sems_z, 5, k - 1, z_peer(k)[1])

    def wait_f(k):
        piece = r.final.at[c, x, 0]
        return copy(piece, piece, r.sems_z, 5, k - 1, z_peer(k)[1])

    def send_xf(piece, k):
        mine = r.final.at[c, x, piece]
        return copy(mine, mine, r.sems_f, k - 1, piece, x_peer(k)[1])

    def start_q(k):
        @pl.when(owns(z_peer(k)[0]))
        def _():
            send_q(k).start()

    each(zs, start_q)

    each(zs, lambda k: gather_z(k).wait_send())
    each(groups, lambda k: push_p(g_peer(k)[0], k).wait_send())
    each(groups, lambda k: push_c(g_peer(k)[0], k).wait_send())
    each(groups, lambda k: push_g(g_peer(k)[0], k).wait_send())
    each(groups, lambda k: gather_g(k).wait_send())
    each(zs, lambda k: push_pz(k).wait_send())
    each(zs, lambda k: push_gz(k).wait_send())
    each(ys, lambda k: col_sums(k).wait_send())
    each(zs, lambda k: gather_f(k).wait_send())
    each(ys, lambda k: spread(k).wait_send())
    each(groups, lambda k: push2(g_peer(k)[0], k).wait_send())
    each(xs, lambda k: send_x(k).wait_send())

    @pl.when(owns(z))
    def _():
        mine = r.quarter[rank(z)]
        each_near(zs, lambda k: wait_q(k).wait_recv())
        for k in range(zs - 1):
            mine = mine + r.zq_in[k].astype(F32)
        r.final[c, x, rank(z)] = mine.astype(BF16)
        each(zs, lambda k: send_f(k).start())
        each(xs, lambda k: send_xf(rank(z), k).start())

    def arrive(k):
        source = lax.rem(z + zs - k, zs)

        @pl.when(owns(source))
        def _():
            wait_f(k).wait_recv()
            each(xs, lambda j: send_xf(rank(source), j).start())

    each_near(zs, arrive)

    def hand_over(k, px):
        piece = r.final.at[c, px]
        return copy(piece, grads.at[c, px], r.sems_x, 1, k, partner)

    def keep(core, px):
        return pltpu.make_async_copy(r.final.at[core, px], grads.at[core, px], r.sems_o.at[core, px])

    hand_over(0, x).start()
    keep(c, x).start()

    def pass_on(k):
        loop(owners, lambda piece: send_xf(piece, k).wait_recv())
        px = lax.rem(x + xs - k, xs)
        hand_over(k, px).start()
        keep(c, px).start()

    each_near(xs, pass_on)

    def finish_q(k):
        @pl.when(owns(z_peer(k)[0]))
        def _():
            wait_q(k).wait_send()

    each(zs, finish_q)

    @pl.when(owns(z))
    def _():
        each(zs, lambda k: wait_f(k).wait_send())

    each(xs, lambda k: loop(owners, lambda piece: send_xf(piece, k).wait_send()))
    loop(xs, lambda q: swap(q).wait_send())
    put_output.wait()

    loop(xs, lambda k: hand_over(k, 0).wait())
    loop(xs, lambda px: keep(c, px).wait())


def finish(output_in, grads_in, output_out, self_out, neigh_out, rows, low, high, sems):
    count, half = low.shape[0], low.shape[1]
    loads = []
    stores = []
    for i in range(count):
        part = pl.ds(i % 2 * half, half)
        target = (self_out, neigh_out)[i // 2]
        loads.append(pltpu.make_async_copy(grads_in.at[i // 2, part], low.at[i], sems.at[0, i]))
        stores.append(pltpu.make_async_copy(high.at[i], target.at[part], sems.at[1, i]))
    loads.append(pltpu.make_async_copy(output_in, rows, sems.at[0, count]))
    stores.append(pltpu.make_async_copy(rows, output_out, sems.at[1, count]))
    for load in loads:
        load.start()
    for i in range(count):
        loads[i].wait()
        high[i] = low[i].astype(F32)
        stores[i].start()
    loads[count].wait()
    stores[count].start()
    for store in stores:
        store.wait()


def local(dims, features, w_self, w_neigh, local_nbr, hub_link, hub_used, cotangent):
    nodes, depth = features.shape
    s = sizes(dims, nodes, depth, w_self.shape[1])
    scratch = scratch_of(s)
    output, grads = pl.pallas_call(
        functools.partial(kernel, s, tuple(scratch)),
        out_shape=(
            jax.ShapeDtypeStruct((nodes, s.width), BF16),
            jax.ShapeDtypeStruct((CORES, s.xs, s.owners, s.o_rows, s.width), BF16),
        ),
        in_specs=[pl.BlockSpec(memory_space=pl.ANY)] * 7,
        out_specs=(pl.BlockSpec(memory_space=pl.ANY),) * 2,
        scratch_shapes=list(scratch.values()),
        compiler_params=pltpu.CompilerParams(
            collective_id=0, has_side_effects=True, vmem_limit_bytes=56 * 1024 * 1024
        ),
    )(features, w_self, w_neigh, local_nbr.T, hub_link.T, hub_used.T, cotangent)
    grad = jax.ShapeDtypeStruct((depth, s.width), F32)
    return pl.pallas_call(
        finish,
        out_shape=(jax.ShapeDtypeStruct((nodes, s.width), BF16), grad, grad),
        in_specs=[pl.BlockSpec(memory_space=pl.ANY)] * 2,
        out_specs=(pl.BlockSpec(memory_space=pl.ANY),) * 3,
        scratch_shapes=[
            pltpu.VMEM((nodes, s.width), BF16),
            pltpu.VMEM((2 * CORES, depth // 2, s.width), BF16),
            pltpu.VMEM((2 * CORES, depth // 2, s.width), F32),
            pltpu.SemaphoreType.DMA((2, 2 * CORES + 1)),
        ],
    )(output, grads.reshape(CORES, depth, s.width))


def solution(mesh):
    ys = mesh.shape["cols"]
    xs = X_CHIPS
    zs = mesh.shape["nodes"] // (xs * CORES)
    placed = (
        P("nodes", None),
        P(None, "cols"),
        P(None, "cols"),
        P("nodes", None),
        P("nodes", None),
        P("nodes", None),
        P("nodes", "cols"),
    )
    return jax.shard_map(
        functools.partial(local, (xs, zs, ys)),
        mesh=mesh,
        in_specs=placed,
        out_specs=(P("nodes", "cols"), P(None, "cols"), P(None, "cols")),
        check_vma=False,
    )
```
